768 devices in a mesh: row: 16 (over y_lo, x, core), col: 48 (over y_hi, z).
Axes of the slice: x: 4, y: 8 (y_hi: 4, y_lo: 2; y = y_hi * 2 + y_lo), z: 12, core: 2. Of those that a mesh axis runs over, the one named last changes fastest.
Arguments:
- tiles: bfloat16 [98304, 4096], P(('row', 'col')), may hold values from -0.25 to 0.25
- tile_row: int32 [98304], P(('row', 'col')), may hold values from 0 to 383
- tile_col: int32 [98304], P(('row', 'col')), may hold values from 0 to 127
- tile_count: int32 [768], P(('row', 'col')), may hold values from 1 to 128, as said below
- block: float32 [8, 393216], P(None, ('row', 'col')), may hold values from -6 to 6
- previous: float32 [8, 393216], P(None, ('row', 'col')), may hold values from -6 to 6
- coupling: float32 [8, 8], replicated, may hold values from -3 to 3
Outputs:
- lanczos_block: float32 [8, 393216], P(None, ('row', 'col'))
- alphas: float32 [2, 8, 8], replicated
The draws below stay inside these ranges and needn't reach their ends.
Inputs may be any that keep to these rules, and one draw needn't show every extreme that they name: tile_count gives how many leading slots of a device are live; some device has exactly 128.
All inputs are finite; a program needn't handle non-finite values.
Results may differ from the reference program's by a relative error of at most 0.0042.
Values may be sent and summed in bfloat16 or wider, within the bound.
No kernel may reach another device: no remote copies, remote signals or barrier semaphores. Data moves between devices by JAX's collectives and lax.ppermute only.
A program may use at most 32 MiB of HBM per device.

```python
import jax
import jax.numpy as jnp
from jax import lax

TILE = 64
NV = 8
SUB = 512
KT = 128
STEPS = 2
N = 393216
ROW_TILES = 384
COL_TILES = 128
N_ROW = 16
N_COL = 48


def draw_tile_count(key, part):
    key = jax.random.fold_in(key, 11)
    first_key, third_key = jax.random.split(key, 2)
    devices_all = N_ROW * N_COL
    counts = jax.random.randint(first_key, (devices_all,), 3 * KT // 4, KT + 1)
    heavy = jax.random.randint(third_key, (), 0, devices_all)
    places = jnp.arange(devices_all, dtype=jnp.int32)
    return jnp.where(places == heavy, KT, counts).astype(jnp.int32)


def plant(drawn, stream_key, low, largest):
    place = [jax.random.randint(jax.random.fold_in(stream_key, axis), (), 0, length) for axis, length in enumerate(drawn.shape)]
    main_axis = drawn.shape.index(max(drawn.shape))
    next_to = place[:main_axis] + [(place[main_axis] + 1) % drawn.shape[main_axis]] + place[main_axis + 1:]
    return drawn.at[tuple(place)].set(low).at[tuple(next_to)].set(largest)


def block_scale(rng, extent, cuts, smallest, largest):
    factor_of = 1.0
    for position, shards_of in cuts:
        heights = jax.random.uniform(jax.random.fold_in(jax.random.fold_in(rng, 6), position), (shards_of,), jnp.float32, smallest / len(cuts), largest / len(cuts))
        factor_of = factor_of * jnp.repeat(jnp.exp(heights), extent[position] // shards_of).reshape((-1,) + (1,) * (len(extent) - 1 - position))
    return factor_of


def normal_values(key, dims, deviation, bound, cuts=(), held_as=jnp.bfloat16):
    entries = jax.random.normal(key, dims, jnp.float32) * deviation
    if len(cuts) > 0:
        entries = block_scale(key, dims, cuts, -0.22, 0.18) * entries
    return jnp.clip(entries, min=-bound, max=bound).astype(held_as)


def setup_inputs(seed: int = 0) -> dict:
    key_list = jax.random.split(jax.random.key(seed), 8)
    return {
        "tiles": normal_values(key_list[0], (N_ROW * N_COL * KT, TILE * TILE), (2048 * KT // SUB) ** -0.5, 0.25, ((0, 768),)),
        "tile_row": plant(jax.random.randint(key_list[1], (N_ROW * N_COL * KT,), 0, ROW_TILES), jax.random.fold_in(key_list[1], 1), 0, ROW_TILES - 1).astype(jnp.int32),
        "tile_col": plant(jax.random.randint(key_list[2], (N_ROW * N_COL * KT,), 0, COL_TILES), jax.random.fold_in(key_list[2], 1), 0, COL_TILES - 1).astype(jnp.int32),
        "tile_count": draw_tile_count(jax.random.fold_in(key_list[7], 71), 0),
        "block": normal_values(key_list[4], (NV, N), 1.0, 6.0, ((1, 768),), jnp.float32),
        "previous": normal_values(key_list[5], (NV, N), 1.0, 6.0, ((1, 768),), jnp.float32),
        "coupling": normal_values(key_list[6], (NV, NV), 0.5, 3.0, (), jnp.float32),
    }


def apply_hamiltonian(vectors, squares, rows, cols, live):
    narrow = vectors.astype(jnp.bfloat16).reshape(NV, N_ROW, N_COL, SUB)
    bands = narrow.transpose(2, 0, 1, 3).reshape(N_COL, NV, N_ROW * SUB)
    across_rows = narrow.reshape(NV, N_ROW, N_COL * SUB).transpose(1, 0, 2)

    def device(sq_d, rw_d, cl_d, lv_d, band_d, across_d):
        picked = band_d.reshape(NV, COL_TILES, TILE)[:, cl_d]
        front = jnp.einsum('kij,vkj->kvi', sq_d.astype(jnp.float32), picked.astype(jnp.float32))
        front = front * lv_d[:, None, None]
        front = jax.ops.segment_sum(front, rw_d, num_segments=ROW_TILES)
        front = front.transpose(1, 0, 2).reshape(NV, N_COL * SUB)
        chosen = across_d.reshape(NV, ROW_TILES, TILE)[:, rw_d]
        back = jnp.einsum('kij,vki->kvj', sq_d.astype(jnp.float32), chosen.astype(jnp.float32))
        back = back * lv_d[:, None, None]
        back = jax.ops.segment_sum(back, cl_d, num_segments=COL_TILES)
        back = back.transpose(1, 0, 2).reshape(NV, N_ROW * SUB)
        return (front, back)

    def one_row(carry, xs):
        sq, rw, cl, lv, across = xs
        fronts, backs = jax.vmap(device, in_axes=(0, 0, 0, 0, 0, None))(sq, rw, cl, lv, bands, across)
        return (carry + backs, jnp.sum(fronts, axis=0))
    start = jnp.zeros((N_COL, NV, N_ROW * SUB), jnp.float32)
    backs, fronts = lax.scan(one_row, start, (squares, rows, cols, live, across_rows))
    front = fronts.transpose(1, 0, 2).reshape(NV, N_ROW * N_COL * SUB)
    back = backs.reshape(N_COL, NV, N_ROW, SUB).transpose(1, 2, 0, 3).reshape(NV, N_ROW * N_COL * SUB)
    return front + back

def reference(tiles, tile_row, tile_col, tile_count, block, previous, coupling):
    total = N_ROW * N_COL * SUB
    squares = tiles.reshape(N_ROW, N_COL, KT, TILE, TILE)
    rows = tile_row.reshape(N_ROW, N_COL, KT)
    cols = tile_col.reshape(N_ROW, N_COL, KT)
    slots = jnp.arange(KT, dtype=jnp.int32)
    live = (slots[None, None, :] < tile_count.reshape(N_ROW, N_COL)[:, :, None]).astype(jnp.float32)
    high = lax.Precision.HIGHEST
    current, prior, beta = (block, previous, coupling)
    found = []
    for step in range(STEPS):
        image = apply_hamiltonian(current, squares, rows, cols, live)
        alpha = jnp.dot(current, image.T, precision=high) / total
        found.append(alpha)
        resid = image - jnp.dot(alpha.T, current, precision=high) - jnp.dot(beta, prior, precision=high)
        gram = jnp.dot(resid, resid.T, precision=high) / total
        lower = jnp.linalg.cholesky(gram)
        following = lax.linalg.triangular_solve(lower, resid, left_side=True, lower=True)
        prior, current, beta = (current, following, lower.T)
    return (current, jnp.stack(found))
```

```python
import functools

import jax
import jax.numpy as jnp
from jax import lax
from jax.experimental import pallas as pl
from jax.experimental.pallas import tpu as pltpu
from jax.sharding import PartitionSpec as P

TILE = 64
NV = 8
STEPS = 2
LANES = 128
GROUP = 16
HIGH = lax.Precision.HIGHEST
F32 = jnp.float32
BF16 = jnp.bfloat16
VMEM = pl.BlockSpec(memory_space=pltpu.VMEM)
SMEM = pl.BlockSpec(memory_space=pltpu.SMEM)
PARAMS = pltpu.CompilerParams(vmem_limit_bytes=40 * 1024 * 1024)


def dot(left, right):
    return jnp.dot(left, right, precision=HIGH, preferred_element_type=F32)


def dot_t(left, right):
    return lax.dot_general(
        left, right, (((1,), (1,)), ((), ())), precision=HIGH, preferred_element_type=F32
    )


def dot_tn(left, right):
    return lax.dot_general(
        left, right, (((0,), (0,)), ((), ())), precision=HIGH, preferred_element_type=F32
    )


def apply_kernel(rows, cols, count, tiles, band, across, front, back, band32, across32, front32):
    slots = tiles.shape[0]
    per_segment = front.shape[2] // TILE
    band32[...] = band[...].astype(F32)
    across32[...] = across[...].astype(F32)
    front32[...] = jnp.zeros_like(front32)
    back[...] = jnp.zeros_like(back)
    half = lax.broadcasted_iota(jnp.int32, (NV, LANES), 1) // TILE

    def place(index):
        within = index % per_segment
        lane = pl.multiple_of(within // 2 * LANES, LANES)
        return index // per_segment, pl.ds(lane, LANES), index % 2

    def group(g, carry):
        updates = []
        for u in range(GROUP):
            k = g * GROUP + u
            live = k < count[0]
            row_segment, row_lanes, row_half = place(rows[k])
            col_segment, col_lanes, col_half = place(cols[k])
            row_mask = half == jnp.where(live, row_half, 2)
            col_mask = half == jnp.where(live, col_half, 2)
            tile = tiles[k]
            picked = jnp.where(col_mask, band32[col_segment, :, col_lanes], 0.0)
            chosen = jnp.where(row_mask, across32[row_segment, :, row_lanes], 0.0)
            chosen = (chosen + pltpu.roll(chosen, TILE, 1))[:, :TILE]
            ahead = lax.dot_general(
                picked.astype(BF16), tile, (((1,), (1,)), ((), ())), preferred_element_type=F32
            )
            behind = jnp.dot(chosen.astype(BF16), tile, preferred_element_type=F32)
            ahead = jnp.where(row_mask, jnp.concatenate([ahead, ahead], axis=1), 0.0)
            behind = jnp.where(col_mask, behind, 0.0)
            updates.append((row_segment, row_lanes, ahead, col_segment, col_lanes, behind))
        for row_segment, row_lanes, ahead, col_segment, col_lanes, behind in updates:
            front32[row_segment, :, row_lanes] += ahead
            back[col_segment, :, col_lanes] += behind
        return carry

    lax.fori_loop(0, slots // GROUP, group, 0)
    front[...] = front32[...].astype(front.dtype)


def apply(rows, cols, count, tiles, band, across):
    return pl.pallas_call(
        apply_kernel,
        out_shape=(
            jax.ShapeDtypeStruct(across.shape, BF16),
            jax.ShapeDtypeStruct(band.shape, F32),
        ),
        in_specs=[SMEM, SMEM, SMEM, VMEM, VMEM, VMEM],
        out_specs=(VMEM, VMEM),
        scratch_shapes=[
            pltpu.VMEM(band.shape, F32),
            pltpu.VMEM(across.shape, F32),
            pltpu.VMEM(across.shape, F32),
        ],
        compiler_params=PARAMS,
        name="apply_tiles",
    )(rows, cols, count, tiles, band, across)


def local_kernel(moved, returned, current, prior, beta, ahead, sums):
    image = jnp.sum(moved[...].astype(F32), axis=0) + jnp.sum(returned[...], axis=0)
    now = current[...]
    rest = image - dot(beta[...], prior[...])
    ahead[...] = rest
    left = jnp.concatenate([now, rest], axis=0)
    right = jnp.concatenate([image, rest, now], axis=0)
    inner = dot_t(left, right)
    pad = jnp.zeros((NV, LANES - 4 * NV), F32)
    one = jnp.concatenate([inner[:NV], inner[NV:, NV : 2 * NV], pad], axis=1)
    sums[...] = jnp.broadcast_to(one[None], sums.shape)


def local(moved, returned, current, prior, beta, n_row):
    return pl.pallas_call(
        local_kernel,
        out_shape=(
            jax.ShapeDtypeStruct(current.shape, F32),
            jax.ShapeDtypeStruct((n_row, NV, LANES), F32),
        ),
        in_specs=[VMEM] * 5,
        out_specs=(VMEM, VMEM),
        compiler_params=PARAMS,
        name="local_sums",
    )(moved, returned, current, prior, beta)


def spread_kernel(parts, sums):
    one = jnp.sum(parts[...], axis=0)
    sums[...] = jnp.broadcast_to(one[None], sums.shape)


def spread(parts, n_col):
    return pl.pallas_call(
        spread_kernel,
        out_shape=jax.ShapeDtypeStruct((n_col, NV, LANES), F32),
        in_specs=[VMEM],
        out_specs=VMEM,
        compiler_params=PARAMS,
        name="spread_sums",
    )(parts)


def next_kernel(total, last, parts, rest, current, alpha_out, upper_out, following, *copies):
    summed = jnp.sum(parts[...], axis=0) / total
    alpha = summed[:, :NV]
    mixed = summed[:, NV : 2 * NV]
    own = summed[:, 2 * NV : 3 * NV]
    square = summed[:, 3 * NV : 4 * NV]
    alpha_out[...] = alpha
    cross = dot_tn(alpha, mixed)
    cross_t = dot_tn(mixed, alpha)
    gram = square - cross - cross_t + dot_tn(alpha, dot(own, alpha))
    row = lax.broadcasted_iota(jnp.int32, (NV, 2 * NV), 0)
    lane = lax.broadcasted_iota(jnp.int32, (NV, 2 * NV), 1)
    unit = jnp.where(row + NV == lane, 1.0, 0.0).astype(F32)
    work = jnp.concatenate([gram, unit[:, NV:]], axis=1)
    for j in range(NV):
        pivot = jnp.sqrt(work[j : j + 1, j : j + 1])
        scaled = work[j : j + 1, :] / pivot
        factor = work[:, j : j + 1] / pivot
        work = jnp.where(row == j, scaled, jnp.where(row > j, work - factor * scaled, work))
    upper_out[...] = jnp.where(row <= lane, work, 0.0)[:, :NV]
    inverse = work[:, NV:]
    resid = rest[...] - dot_tn(alpha, current[...])
    block = dot(inverse, resid)
    following[...] = block
    if not last:
        narrow = block.astype(BF16)
        for copy in copies:
            copy[...] = jnp.broadcast_to(narrow[None], copy.shape)


def advance(parts, rest, current, total, n_row, n_col, last):
    sub = current.shape[1]
    shapes = [
        jax.ShapeDtypeStruct((NV, NV), F32),
        jax.ShapeDtypeStruct((NV, NV), F32),
        jax.ShapeDtypeStruct(current.shape, F32),
    ]
    if not last:
        shapes.append(jax.ShapeDtypeStruct((n_row, NV, sub), BF16))
        shapes.append(jax.ShapeDtypeStruct((n_col, NV, sub), BF16))
    return pl.pallas_call(
        functools.partial(next_kernel, total, last),
        out_shape=tuple(shapes),
        in_specs=[VMEM] * 3,
        out_specs=(VMEM,) * len(shapes),
        compiler_params=PARAMS,
        name="next_block",
    )(parts, rest, current)


def swap(blocks, axis):
    return lax.all_to_all(blocks, axis, 0, 0, tiled=True)


def shards(tiles, tile_row, tile_col, tile_count, block, previous, coupling):
    slots = tiles.shape[0]
    sub = block.shape[1]
    n_row = lax.axis_size("row")
    n_col = lax.axis_size("col")
    total = float(sub * n_row * n_col)
    squares = tiles.reshape(slots, TILE, TILE)
    squares = jnp.concatenate([squares, squares], axis=2)
    current, prior, beta = (block, previous, coupling)
    narrow = current.astype(BF16)
    to_row = jnp.broadcast_to(narrow[None], (n_row, NV, sub))
    to_col = jnp.broadcast_to(narrow[None], (n_col, NV, sub))
    found = []
    for step in range(STEPS):
        last = step == STEPS - 1
        band = swap(to_row, "row")
        across = swap(to_col, "col")
        front, back = apply(tile_row, tile_col, tile_count, squares, band, across)
        moved = swap(front, "col")
        returned = swap(back, "row")
        rest, sums = local(moved, returned, current, prior, beta, n_row)
        sums = spread(swap(sums, "row"), n_col)
        parts = swap(sums, "col")
        alpha, upper, following, *copies = advance(
            parts, rest, current, total, n_row, n_col, last
        )
        found.append(alpha)
        if not last:
            to_row, to_col = copies
        prior, current, beta = (current, following, upper)
    return (current, jnp.stack(found))


def solution(mesh):
    in_specs = (
        P(("row", "col"), None),
        P(("row", "col")),
        P(("row", "col")),
        P(("row", "col")),
        P(None, ("row", "col")),
        P(None, ("row", "col")),
        P(),
    )
    out_specs = (P(None, ("row", "col")), P())
    return jax.shard_map(shards, mesh=mesh, in_specs=in_specs, out_specs=out_specs, check_vma=False)
```

```python
import functools

import jax
import jax.numpy as jnp
from jax import lax
from jax.experimental import pallas as pl
from jax.experimental.pallas import tpu as pltpu
from jax.sharding import PartitionSpec as P

TILE = 64
NV = 8
STEPS = 2
LANES = 128
GROUP = 16
HIGH = lax.Precision.HIGHEST
F32 = jnp.float32
BF16 = jnp.bfloat16
VMEM = pl.BlockSpec(memory_space=pltpu.VMEM)
SMEM = pl.BlockSpec(memory_space=pltpu.SMEM)
PARAMS = pltpu.CompilerParams(vmem_limit_bytes=40 * 1024 * 1024)


def dot(left, right):
    return jnp.dot(left, right, precision=HIGH, preferred_element_type=F32)


def dot_t(left, right):
    return lax.dot_general(
        left, right, (((1,), (1,)), ((), ())), precision=HIGH, preferred_element_type=F32
    )


def dot_tn(left, right):
    return lax.dot_general(
        left, right, (((0,), (0,)), ((), ())), precision=HIGH, preferred_element_type=F32
    )


def place(index, per_segment):
    within = index % per_segment
    lane = pl.multiple_of(within // 2 * LANES, LANES)
    return index // per_segment, pl.ds(lane, LANES), index % 2


def lane_half():
    return lax.broadcasted_iota(jnp.int32, (NV, LANES), 1) // TILE


def narrowed(pair, mask):
    held = jnp.where(mask, pair, 0.0)
    return (held + pltpu.roll(held, TILE, 1))[:, :TILE].astype(BF16)


def both_halves(product, mask):
    return jnp.where(mask, jnp.concatenate([product, product], axis=1), 0.0)


def front_kernel(rows, cols, count, tiles, band, narrow, message, band32, front32):
    slots = tiles.shape[0]
    per_segment = message.shape[2] // TILE
    band32[...] = band[...].astype(F32)
    front32[...] = jnp.zeros_like(front32)
    half = lane_half()

    def group(g, carry):
        updates = []
        for u in range(GROUP):
            k = g * GROUP + u
            row_segment, row_lanes, row_half = place(rows[k], per_segment)
            col_segment, col_lanes, col_half = place(cols[k], per_segment)
            col_mask = half == jnp.where(k < count[0], col_half, 2)
            picked = narrowed(band32[col_segment, :, col_lanes], col_mask)
            ahead = lax.dot_general(
                picked, tiles[k], (((1,), (1,)), ((), ())), preferred_element_type=F32
            )
            updates.append((row_segment, row_lanes, both_halves(ahead, half == row_half)))
        for segment, lanes, ahead in updates:
            front32[segment, :, lanes] += ahead
        return carry

    lax.fori_loop(0, slots // GROUP, group, 0)
    own = jnp.broadcast_to(narrow[...][None], (message.shape[0],) + narrow.shape)
    message[...] = jnp.concatenate([own, front32[...].astype(BF16)], axis=1)


def front(rows, cols, count, tiles, band, narrow, n_col):
    sub = band.shape[2]
    return pl.pallas_call(
        front_kernel,
        out_shape=jax.ShapeDtypeStruct((n_col, 2 * NV, sub), BF16),
        in_specs=[SMEM, SMEM, SMEM, VMEM, VMEM, VMEM],
        out_specs=VMEM,
        scratch_shapes=[pltpu.VMEM(band.shape, F32), pltpu.VMEM((n_col, NV, sub), F32)],
        compiler_params=PARAMS,
        name="front_tiles",
    )(rows, cols, count, tiles, band, narrow)


def back_kernel(rows, cols, count, tiles, moved, back, owned, across32):
    slots = tiles.shape[0]
    per_segment = moved.shape[2] // TILE
    arrived = moved[...].astype(F32)
    across32[...] = arrived[:, :NV]
    owned[...] = jnp.sum(arrived[:, NV:], axis=0)
    back[...] = jnp.zeros_like(back)
    half = lane_half()

    def group(g, carry):
        updates = []
        for u in range(GROUP):
            k = g * GROUP + u
            row_segment, row_lanes, row_half = place(rows[k], per_segment)
            col_segment, col_lanes, col_half = place(cols[k], per_segment)
            row_mask = half == jnp.where(k < count[0], row_half, 2)
            chosen = narrowed(across32[row_segment, :, row_lanes], row_mask)
            behind = jnp.dot(chosen, tiles[k], preferred_element_type=F32)
            updates.append((col_segment, col_lanes, both_halves(behind, half == col_half)))
        for segment, lanes, behind in updates:
            back[segment, :, lanes] += behind
        return carry

    lax.fori_loop(0, slots // GROUP, group, 0)


def back(rows, cols, count, tiles, moved, n_row):
    sub = moved.shape[2]
    return pl.pallas_call(
        back_kernel,
        out_shape=(
            jax.ShapeDtypeStruct((n_row, NV, sub), F32),
            jax.ShapeDtypeStruct((NV, sub), F32),
        ),
        in_specs=[SMEM, SMEM, SMEM, VMEM, VMEM],
        out_specs=(VMEM, VMEM),
        scratch_shapes=[pltpu.VMEM((moved.shape[0], NV, sub), F32)],
        compiler_params=PARAMS,
        name="back_tiles",
    )(rows, cols, count, tiles, moved)


def local_kernel(owned, returned, current, prior, beta, ahead, sums):
    image = owned[...] + jnp.sum(returned[...], axis=0)
    now = current[...]
    rest = image - dot(beta[...], prior[...])
    ahead[...] = rest
    left = jnp.concatenate([now, rest], axis=0)
    right = jnp.concatenate([image, rest, now], axis=0)
    inner = dot_t(left, right)
    blocks = jnp.concatenate([inner[:NV], inner[NV:, NV : 2 * NV]], axis=1)
    packed = [
        jnp.concatenate([blocks[v : v + 1] for v in range(part, part + 4)], axis=1)
        for part in (0, 4)
    ]
    one = jnp.concatenate(packed, axis=0)
    sums[...] = jnp.broadcast_to(one[None], sums.shape)


def local(owned, returned, current, prior, beta, n_row):
    return pl.pallas_call(
        local_kernel,
        out_shape=(
            jax.ShapeDtypeStruct(current.shape, F32),
            jax.ShapeDtypeStruct((n_row, 2, LANES), F32),
        ),
        in_specs=[VMEM] * 5,
        out_specs=(VMEM, VMEM),
        compiler_params=PARAMS,
        name="local_sums",
    )(owned, returned, current, prior, beta)


def spread_kernel(parts, sums):
    one = jnp.sum(parts[...], axis=0)
    sums[...] = jnp.broadcast_to(one[None], sums.shape)


def spread(parts, n_col):
    return pl.pallas_call(
        spread_kernel,
        out_shape=jax.ShapeDtypeStruct((n_col, 2, LANES), F32),
        in_specs=[VMEM],
        out_specs=VMEM,
        compiler_params=PARAMS,
        name="spread_sums",
    )(parts)


def next_kernel(total, last, parts, rest, current, alpha_out, upper_out, following, *sent):
    packed = jnp.sum(parts[...], axis=0) / total
    width = LANES // 4
    summed = jnp.concatenate(
        [packed[v // 4 : v // 4 + 1, v % 4 * width : (v % 4 + 1) * width] for v in range(NV)],
        axis=0,
    )
    alpha = summed[:, :NV]
    mixed = summed[:, NV : 2 * NV]
    own = summed[:, 2 * NV : 3 * NV]
    square = summed[:, 3 * NV : 4 * NV]
    alpha_out[...] = alpha
    cross = dot_tn(alpha, mixed)
    cross_t = dot_tn(mixed, alpha)
    gram = square - cross - cross_t + dot_tn(alpha, dot(own, alpha))
    row = lax.broadcasted_iota(jnp.int32, (NV, 2 * NV), 0)
    lane = lax.broadcasted_iota(jnp.int32, (NV, 2 * NV), 1)
    unit = jnp.where(row + NV == lane, 1.0, 0.0).astype(F32)
    work = jnp.concatenate([gram, unit[:, NV:]], axis=1)
    for j in range(NV):
        pivot = jnp.sqrt(work[j : j + 1, j : j + 1])
        scaled = work[j : j + 1, :] / pivot
        factor = work[:, j : j + 1] / pivot
        work = jnp.where(row == j, scaled, jnp.where(row > j, work - factor * scaled, work))
    upper_out[...] = jnp.where(row <= lane, work, 0.0)[:, :NV]
    inverse = work[:, NV:]
    resid = rest[...] - dot_tn(alpha, current[...])
    block = dot(inverse, resid)
    following[...] = block
    if not last:
        narrow = block.astype(BF16)
        to_row, own = sent
        to_row[...] = jnp.broadcast_to(narrow[None], to_row.shape)
        own[...] = narrow


def advance(parts, rest, current, total, n_row, last):
    sub = current.shape[1]
    shapes = [
        jax.ShapeDtypeStruct((NV, NV), F32),
        jax.ShapeDtypeStruct((NV, NV), F32),
        jax.ShapeDtypeStruct(current.shape, F32),
    ]
    if not last:
        shapes.append(jax.ShapeDtypeStruct((n_row, NV, sub), BF16))
        shapes.append(jax.ShapeDtypeStruct((NV, sub), BF16))
    return pl.pallas_call(
        functools.partial(next_kernel, total, last),
        out_shape=tuple(shapes),
        in_specs=[VMEM] * 3,
        out_specs=(VMEM,) * len(shapes),
        compiler_params=PARAMS,
        name="next_block",
    )(parts, rest, current)


def swap(blocks, axis):
    return lax.all_to_all(blocks, axis, 0, 0, tiled=True)


def shards(tiles, tile_row, tile_col, tile_count, block, previous, coupling):
    slots = tiles.shape[0]
    sub = block.shape[1]
    n_row = lax.axis_size("row")
    n_col = lax.axis_size("col")
    total = float(sub * n_row * n_col)
    squares = tiles.reshape(slots, TILE, TILE)
    current, prior, beta = (block, previous, coupling)
    narrow = current.astype(BF16)
    to_row = jnp.broadcast_to(narrow[None], (n_row, NV, sub))
    found = []
    for step in range(STEPS):
        last = step == STEPS - 1
        band = swap(to_row, "row")
        message = front(tile_row, tile_col, tile_count, squares, band, narrow, n_col)
        moved = swap(message, "col")
        partial, owned = back(tile_row, tile_col, tile_count, squares, moved, n_row)
        returned = swap(partial, "row")
        rest, sums = local(owned, returned, current, prior, beta, n_row)
        sums = spread(swap(sums, "row"), n_col)
        parts = swap(sums, "col")
        alpha, upper, following, *sent = advance(parts, rest, current, total, n_row, last)
        found.append(alpha)
        if not last:
            to_row, narrow = sent
        prior, current, beta = (current, following, upper)
    return (current, jnp.stack(found))


def solution(mesh):
    in_specs = (
        P(("row", "col"), None),
        P(("row", "col")),
        P(("row", "col")),
        P(("row", "col")),
        P(None, ("row", "col")),
        P(None, ("row", "col")),
        P(),
    )
    out_specs = (P(None, ("row", "col")), P())
    return jax.shard_map(shards, mesh=mesh, in_specs=in_specs, out_specs=out_specs, check_vma=False)
```

```python
import functools

import jax
import jax.numpy as jnp
from jax import lax
from jax.experimental import pallas as pl
from jax.experimental.pallas import tpu as pltpu
from jax.sharding import PartitionSpec as P

TILE = 64
NV = 8
STEPS = 2
LANES = 128
GROUP = 32
DEPTH = 12
BOTH = ("row", "col")
HIGH = lax.Precision.HIGHEST
F32 = jnp.float32
BF16 = jnp.bfloat16
VMEM = pl.BlockSpec(memory_space=pltpu.VMEM)
SMEM = pl.BlockSpec(memory_space=pltpu.SMEM)
PARAMS = pltpu.CompilerParams(vmem_limit_bytes=40 * 1024 * 1024)


def dot(left, right):
    return jnp.dot(left, right, precision=HIGH, preferred_element_type=F32)


def dot_t(left, right):
    return lax.dot_general(
        left, right, (((1,), (1,)), ((), ())), precision=HIGH, preferred_element_type=F32
    )


def dot_tn(left, right):
    return lax.dot_general(
        left, right, (((0,), (0,)), ((), ())), precision=HIGH, preferred_element_type=F32
    )


def lane_half():
    return lax.broadcasted_iota(jnp.int32, (NV, LANES), 1) // TILE


def narrowed(pair, mask):
    held = jnp.where(mask, pair, 0.0)
    return (held + pltpu.roll(held, TILE, 1))[:, :TILE].astype(BF16)


def both_halves(product, mask):
    return jnp.where(mask, jnp.concatenate([product, product], axis=1), 0.0)


def to_pairs(segments, pairs):
    count, _, sub = segments.shape
    per = sub // LANES
    for segment in range(count):
        held = segments[segment, :NV].astype(F32)
        for part in range(per):
            pairs[segment * per + part] = held[:, part * LANES : (part + 1) * LANES]
    pairs[count * per] = jnp.zeros((NV, LANES), F32)


def segment_of(pairs, segment, per):
    parts = [pairs[segment * per + part] for part in range(per)]
    return jnp.concatenate(parts, axis=1)


def pair_scratch(count, sub):
    return pltpu.VMEM((count * sub // LANES + 1, NV, LANES), F32)


def accumulate(reads, writes, tiles, pairs, sums, product):
    half = lane_half()
    sums[...] = jnp.zeros_like(sums)

    def group(g, carry):
        updates = []
        for u in range(GROUP):
            k = g * GROUP + u
            read, write = reads[k], writes[k]
            picked = narrowed(pairs[lax.shift_right_logical(read, 1)], half == (read & 1))
            out = both_halves(product(picked, tiles[k]), half == (write & 1))
            updates.append((lax.shift_right_logical(write, 1), out))
        for pair, out in updates:
            sums[pair] += out
        return carry

    lax.fori_loop(0, tiles.shape[0] // GROUP, group, 0)


def front_kernel(rows, cols, tiles, band, narrow, message, band_pairs, sums):
    to_pairs(band, band_pairs)

    def product(picked, tile):
        return lax.dot_general(
            picked, tile, (((1,), (1,)), ((), ())), preferred_element_type=F32
        )

    accumulate(cols, rows, tiles, band_pairs, sums, product)
    per = message.shape[2] // LANES
    own = narrow[...]
    for segment in range(message.shape[0]):
        partial = segment_of(sums, segment, per).astype(BF16)
        message[segment] = jnp.concatenate([own, partial], axis=0)


def front(rows, cols, tiles, band, narrow, n_col):
    n_row, _, sub = band.shape
    return pl.pallas_call(
        front_kernel,
        out_shape=jax.ShapeDtypeStruct((n_col, 2 * NV, sub), BF16),
        in_specs=[SMEM, SMEM, VMEM, VMEM, VMEM],
        out_specs=VMEM,
        scratch_shapes=[pair_scratch(n_row, sub), pair_scratch(n_col, sub)],
        compiler_params=PARAMS,
        name="front_tiles",
    )(rows, cols, tiles, band, narrow)


def back_kernel(rows, cols, tiles, moved, back, owned, across_pairs, sums):
    to_pairs(moved, across_pairs)
    owned[...] = jnp.sum(moved[:, NV:].astype(F32), axis=0)

    def product(picked, tile):
        return jnp.dot(picked, tile, preferred_element_type=F32)

    accumulate(rows, cols, tiles, across_pairs, sums, product)
    per = back.shape[2] // LANES
    for segment in range(back.shape[0]):
        back[segment] = segment_of(sums, segment, per)


def back(rows, cols, tiles, moved, n_row):
    n_col, _, sub = moved.shape
    return pl.pallas_call(
        back_kernel,
        out_shape=(
            jax.ShapeDtypeStruct((n_row, NV, sub), F32),
            jax.ShapeDtypeStruct((NV, sub), F32),
        ),
        in_specs=[SMEM, SMEM, VMEM, VMEM],
        out_specs=(VMEM, VMEM),
        scratch_shapes=[pair_scratch(n_col, sub), pair_scratch(n_row, sub)],
        compiler_params=PARAMS,
        name="back_tiles",
    )(rows, cols, tiles, moved)


def local_kernel(owned, returned, current, prior, beta, ahead, sums):
    image = owned[...] + jnp.sum(returned[...], axis=0)
    now = current[...]
    rest = image - dot(beta[...], prior[...])
    ahead[...] = rest
    left = jnp.concatenate([now, rest], axis=0)
    right = jnp.concatenate([image, rest, now], axis=0)
    inner = dot_t(left, right)
    blocks = jnp.concatenate([inner[:NV], inner[NV:, NV : 2 * NV]], axis=1)
    packed = [
        jnp.concatenate([blocks[v : v + 1] for v in range(part, part + 4)], axis=1)
        for part in (0, 4)
    ]
    one = jnp.concatenate(packed, axis=0)
    sums[...] = jnp.broadcast_to(one[None], sums.shape)


def local(owned, returned, current, prior, beta, copies):
    return pl.pallas_call(
        local_kernel,
        out_shape=(
            jax.ShapeDtypeStruct(current.shape, F32),
            jax.ShapeDtypeStruct((copies, 2, LANES), F32),
        ),
        in_specs=[VMEM] * 5,
        out_specs=(VMEM, VMEM),
        compiler_params=PARAMS,
        name="local_sums",
    )(owned, returned, current, prior, beta)


def spread_kernel(parts, sums):
    one = jnp.sum(parts[...], axis=0)
    sums[...] = jnp.broadcast_to(one[None], sums.shape)


def spread(parts, copies):
    return pl.pallas_call(
        spread_kernel,
        out_shape=jax.ShapeDtypeStruct((copies, 2, LANES), F32),
        in_specs=[VMEM],
        out_specs=VMEM,
        compiler_params=PARAMS,
        name="spread_sums",
    )(parts)


def next_kernel(total, step, last, parts, rest, current, found, alphas, upper_out, following, *sent):
    packed = jnp.sum(parts[...], axis=0) / total
    width = LANES // 4
    summed = jnp.concatenate(
        [packed[v // 4 : v // 4 + 1, v % 4 * width : (v % 4 + 1) * width] for v in range(NV)],
        axis=0,
    )
    alpha = summed[:, :NV]
    mixed = summed[:, NV : 2 * NV]
    own = summed[:, 2 * NV : 3 * NV]
    square = summed[:, 3 * NV : 4 * NV]
    alphas[...] = found[...]
    alphas[step] = alpha
    cross = dot_tn(alpha, mixed)
    cross_t = dot_tn(mixed, alpha)
    gram = square - cross - cross_t + dot_tn(alpha, dot(own, alpha))
    row = lax.broadcasted_iota(jnp.int32, (NV, 2 * NV), 0)
    lane = lax.broadcasted_iota(jnp.int32, (NV, 2 * NV), 1)
    unit = jnp.where(row + NV == lane, 1.0, 0.0).astype(F32)
    work = jnp.concatenate([gram, unit[:, NV:]], axis=1)
    for j in range(NV):
        pivot = jnp.sqrt(work[j : j + 1, j : j + 1])
        scaled = work[j : j + 1, :] / pivot
        factor = work[:, j : j + 1] / pivot
        work = jnp.where(row == j, scaled, jnp.where(row > j, work - factor * scaled, work))
    upper_out[...] = jnp.where(row <= lane, work, 0.0)[:, :NV]
    inverse = work[:, NV:]
    resid = rest[...] - dot_tn(alpha, current[...])
    block = dot(inverse, resid)
    following[...] = block
    if not last:
        narrow = block.astype(BF16)
        to_row, own = sent
        to_row[...] = jnp.broadcast_to(narrow[None], to_row.shape)
        own[...] = narrow


def advance(parts, rest, current, found, total, n_row, step, last):
    sub = current.shape[1]
    shapes = [
        jax.ShapeDtypeStruct(found.shape, F32),
        jax.ShapeDtypeStruct((NV, NV), F32),
        jax.ShapeDtypeStruct(current.shape, F32),
    ]
    if not last:
        shapes.append(jax.ShapeDtypeStruct((n_row, NV, sub), BF16))
        shapes.append(jax.ShapeDtypeStruct((NV, sub), BF16))
    return pl.pallas_call(
        functools.partial(next_kernel, total, step, last),
        out_shape=tuple(shapes),
        in_specs=[VMEM] * 4,
        out_specs=(VMEM,) * len(shapes),
        compiler_params=PARAMS,
        name="next_block",
    )(parts, rest, current, found)


def swap(blocks, axis, groups=None):
    return lax.all_to_all(blocks, axis, 0, 0, tiled=True, axis_index_groups=groups)


def planes_and_lines(n_row, n_col):
    depth = DEPTH if n_col % DEPTH == 0 else n_col
    lines = [
        [row * n_col + high * depth + z for z in range(depth)]
        for row in range(n_row)
        for high in range(n_col // depth)
    ]
    planes = [[line[z] for line in lines] for z in range(depth)]
    return planes, lines


def shards(tiles, tile_row, tile_col, tile_count, block, previous, coupling):
    slots = tiles.shape[0]
    sub = block.shape[1]
    n_row = lax.axis_size("row")
    n_col = lax.axis_size("col")
    total = float(sub * n_row * n_col)
    squares = tiles.reshape(slots, TILE, TILE)
    current, prior, beta = (block, previous, coupling)
    narrow = current.astype(BF16)
    to_row = jnp.broadcast_to(narrow[None], (n_row, NV, sub))
    live = lax.iota(jnp.int32, slots) < tile_count[0]
    rows = jnp.where(live, tile_row, n_col * sub // TILE)
    cols = jnp.where(live, tile_col, n_row * sub // TILE)
    planes, lines = planes_and_lines(n_row, n_col)
    found = jnp.zeros((STEPS, NV, NV), F32)
    for step in range(STEPS):
        last = step == STEPS - 1
        band = swap(to_row, "row")
        moved = swap(front(rows, cols, squares, band, narrow, n_col), "col")
        partial, owned = back(rows, cols, squares, moved, n_row)
        returned = swap(partial, "row")
        rest, sums = local(owned, returned, current, prior, beta, len(planes[0]))
        sums = spread(swap(sums, BOTH, planes), len(lines[0]))
        parts = swap(sums, BOTH, lines)
        found, upper, following, *sent = advance(
            parts, rest, current, found, total, n_row, step, last
        )
        if not last:
            to_row, narrow = sent
        prior, current, beta = (current, following, upper)
    return (current, found)


def solution(mesh):
    in_specs = (
        P(("row", "col"), None),
        P(("row", "col")),
        P(("row", "col")),
        P(("row", "col")),
        P(None, ("row", "col")),
        P(None, ("row", "col")),
        P(),
    )
    out_specs = (P(None, ("row", "col")), P())
    return jax.shard_map(shards, mesh=mesh, in_specs=in_specs, out_specs=out_specs, check_vma=False)
```

```python
import functools

import jax
import jax.numpy as jnp
from jax import lax
from jax.experimental import pallas as pl
from jax.experimental.pallas import tpu as pltpu
from jax.sharding import PartitionSpec as P

TILE = 64
NV = 8
STEPS = 2
LANES = 128
GROUP = 32
DEPTH = 12
BOTH = ("row", "col")
AHEAD = (((1,), (1,)), ((), ()))
BEHIND = (((1,), (0,)), ((), ()))
HIGH = lax.Precision.HIGHEST
F32 = jnp.float32
BF16 = jnp.bfloat16
VMEM = pl.BlockSpec(memory_space=pltpu.VMEM)
SMEM = pl.BlockSpec(memory_space=pltpu.SMEM)
PARAMS = pltpu.CompilerParams(vmem_limit_bytes=40 * 1024 * 1024)


def dot(left, right):
    return jnp.dot(left, right, precision=HIGH, preferred_element_type=F32)


def dot_t(left, right):
    return lax.dot_general(
        left, right, (((1,), (1,)), ((), ())), precision=HIGH, preferred_element_type=F32
    )


def dot_tn(left, right):
    return lax.dot_general(
        left, right, (((0,), (0,)), ((), ())), precision=HIGH, preferred_element_type=F32
    )


def lane_half():
    return lax.broadcasted_iota(jnp.int32, (NV, LANES), 1) // TILE


def narrowed(pair, mask):
    held = jnp.where(mask, pair, 0.0)
    return (held + pltpu.roll(held, TILE, 1))[:, :TILE]


def pieces(value, count):
    found = []
    for _ in range(count):
        piece = value.astype(BF16)
        value = value - piece.astype(F32)
        found.append(piece)
    return found


def product_of(picked, tile, dims, split):
    if split == 1:
        return lax.dot_general(picked.astype(BF16), tile, dims, preferred_element_type=F32)
    both = jnp.concatenate(pieces(picked, 2), axis=0)
    out = lax.dot_general(both, tile, dims, preferred_element_type=F32)
    return out[:NV] + out[NV:]


def both_halves(product, mask):
    return jnp.where(mask, jnp.concatenate([product, product], axis=1), 0.0)


def mix(coefficients, rows):
    out = coefficients[:, 0:1] * rows[0:1]
    for v in range(1, NV):
        out = out + coefficients[:, v : v + 1] * rows[v : v + 1]
    return out


def factor(gram):
    row = lax.broadcasted_iota(jnp.int32, (NV, 2 * NV), 0)
    lane = lax.broadcasted_iota(jnp.int32, (NV, 2 * NV), 1)
    unit = jnp.where(row + NV == lane, 1.0, 0.0).astype(F32)
    work = jnp.concatenate([gram, unit[:, NV:]], axis=1)
    for j in range(NV):
        pivot = jnp.sqrt(work[j : j + 1, j : j + 1])
        scaled = work[j : j + 1, :] / pivot
        column = work[:, j : j + 1] / pivot
        work = jnp.where(row == j, scaled, jnp.where(row > j, work - column * scaled, work))
    return jnp.where(row <= lane, work, 0.0)[:, :NV], work[:, NV:]


def factor_of_sums(summed):
    alpha = summed[:, :NV]
    mixed = summed[:, NV : 2 * NV]
    own = summed[:, 2 * NV : 3 * NV]
    square = summed[:, 3 * NV : 4 * NV]
    gram = square - dot_tn(alpha, mixed) - dot_tn(mixed, alpha) + dot_tn(alpha, dot(own, alpha))
    return (alpha, *factor(gram))


def identity():
    row = lax.broadcasted_iota(jnp.int32, (NV, NV), 0)
    lane = lax.broadcasted_iota(jnp.int32, (NV, NV), 1)
    return jnp.where(row == lane, 1.0, 0.0).astype(F32)


def put_pairs(held, segment, pairs):
    per = held.shape[1] // LANES
    for part in range(per):
        pairs[segment * per + part] = held[:, part * LANES : (part + 1) * LANES]


def end_pairs(pairs):
    pairs[pairs.shape[0] - 1] = jnp.zeros((NV, LANES), F32)


def to_pairs(segments, pairs):
    for segment in range(segments.shape[0]):
        put_pairs(segments[segment, :NV].astype(F32), segment, pairs)
    end_pairs(pairs)


def segment_of(pairs, segment, per):
    parts = [pairs[segment * per + part] for part in range(per)]
    return jnp.concatenate(parts, axis=1)


def pair_scratch(count, sub):
    return pltpu.VMEM((count * sub // LANES + 1, NV, LANES), F32)


def accumulate(reads, writes, tiles, pairs, sums, dims, split=1):
    half = lane_half()
    sums[...] = jnp.zeros_like(sums)

    def group(g, carry):
        updates = []
        for u in range(GROUP):
            k = g * GROUP + u
            read, write = reads[k], writes[k]
            picked = narrowed(pairs[lax.shift_right_logical(read, 1)], half == (read & 1))
            out = both_halves(product_of(picked, tiles[k], dims, split), half == (write & 1))
            updates.append((lax.shift_right_logical(write, 1), out))
        for pair, out in updates:
            sums[pair] += out
        return carry

    lax.fori_loop(0, tiles.shape[0] // GROUP, group, 0)


def front_kernel(rows, cols, tiles, band, narrow, message, band_pairs, sums):
    to_pairs(band, band_pairs)
    accumulate(cols, rows, tiles, band_pairs, sums, AHEAD)
    per = message.shape[2] // LANES
    own = narrow[...]
    for segment in range(message.shape[0]):
        partial = segment_of(sums, segment, per).astype(BF16)
        message[segment] = jnp.concatenate([own, partial], axis=0)


def front(rows, cols, tiles, band, narrow, n_col):
    n_row, _, sub = band.shape
    return pl.pallas_call(
        front_kernel,
        out_shape=jax.ShapeDtypeStruct((n_col, 2 * NV, sub), BF16),
        in_specs=[SMEM, SMEM, VMEM, VMEM, VMEM],
        out_specs=VMEM,
        scratch_shapes=[pair_scratch(n_row, sub), pair_scratch(n_col, sub)],
        compiler_params=PARAMS,
        name="front_tiles",
    )(rows, cols, tiles, band, narrow)


def back_kernel(rows, cols, tiles, moved, back, owned, across_pairs, sums):
    to_pairs(moved, across_pairs)
    owned[...] = jnp.sum(moved[:, NV:].astype(F32), axis=0)
    accumulate(rows, cols, tiles, across_pairs, sums, BEHIND)
    per = back.shape[2] // LANES
    for segment in range(back.shape[0]):
        back[segment] = segment_of(sums, segment, per)


def back(rows, cols, tiles, moved, n_row):
    n_col, _, sub = moved.shape
    return pl.pallas_call(
        back_kernel,
        out_shape=(
            jax.ShapeDtypeStruct((n_row, NV, sub), F32),
            jax.ShapeDtypeStruct((NV, sub), F32),
        ),
        in_specs=[SMEM, SMEM, VMEM, VMEM],
        out_specs=(VMEM, VMEM),
        scratch_shapes=[pair_scratch(n_col, sub), pair_scratch(n_row, sub)],
        compiler_params=PARAMS,
        name="back_tiles",
    )(rows, cols, tiles, moved)


def rest_and_sums(owned, returned, current, prior, beta):
    image = owned[...] + jnp.sum(returned[...], axis=0)
    now = current[...]
    rest = image - dot(beta[...], prior[...])
    left = jnp.concatenate([now, rest], axis=0)
    right = jnp.concatenate([image, rest, now], axis=0)
    inner = dot_t(left, right)
    return rest, jnp.concatenate([inner[:NV], inner[NV:, NV : 2 * NV]], axis=1)


def local_kernel(owned, returned, current, prior, beta, ahead, sums):
    rest, blocks = rest_and_sums(owned, returned, current, prior, beta)
    ahead[...] = rest
    packed = [
        jnp.concatenate([blocks[v : v + 1] for v in range(part, part + 4)], axis=1)
        for part in (0, 4)
    ]
    one = jnp.concatenate(packed, axis=0)
    sums[...] = jnp.broadcast_to(one[None], sums.shape)


def local(owned, returned, current, prior, beta, copies):
    return pl.pallas_call(
        local_kernel,
        out_shape=(
            jax.ShapeDtypeStruct(current.shape, F32),
            jax.ShapeDtypeStruct((copies, 2, LANES), F32),
        ),
        in_specs=[VMEM] * 5,
        out_specs=(VMEM, VMEM),
        compiler_params=PARAMS,
        name="local_sums",
    )(owned, returned, current, prior, beta)


def carry_kernel(owned, returned, current, prior, beta, ahead, message):
    rest, blocks = rest_and_sums(owned, returned, current, prior, beta)
    ahead[...] = rest
    pad = jnp.zeros((NV, LANES - 4 * NV), F32)
    one = jnp.concatenate([rest, blocks, pad], axis=1)
    message[...] = jnp.broadcast_to(one[None], message.shape)


def carry(owned, returned, current, prior, beta, n_row):
    sub = current.shape[1]
    return pl.pallas_call(
        carry_kernel,
        out_shape=(
            jax.ShapeDtypeStruct(current.shape, F32),
            jax.ShapeDtypeStruct((n_row, NV, sub + LANES), F32),
        ),
        in_specs=[VMEM] * 5,
        out_specs=(VMEM, VMEM),
        compiler_params=PARAMS,
        name="local_carry",
    )(owned, returned, current, prior, beta)


def whiten_kernel(rows, cols, tiles, got, rest, message, band_pairs, sums):
    n_row = got.shape[0]
    sub = rest.shape[1]
    summed = jnp.sum(got[:, :, sub:], axis=0)[:, : 4 * NV]
    gram = summed[:, 3 * NV :] / float(n_row * sub)
    unit = identity()
    trace = jnp.sum(jnp.sum(gram * unit, axis=1, keepdims=True), axis=0, keepdims=True)
    upper, inverse = factor(gram + (trace * 1e-5 + 1e-30) * unit)
    lower = dot_tn(upper, unit)
    for segment in range(n_row):
        put_pairs(mix(inverse, got[segment, :, :sub]), segment, band_pairs)
    end_pairs(band_pairs)
    own = mix(inverse, rest[...]).astype(BF16)
    wide = jnp.concatenate([lower, jnp.zeros((NV, 3 * NV), F32)], axis=1)
    held = jnp.concatenate([summed, wide], axis=0)
    beside = jnp.concatenate(pieces(held, 3) + [jnp.zeros((2 * NV, 4 * NV), BF16)], axis=1)
    accumulate(cols, rows, tiles, band_pairs, sums, AHEAD)
    per = sub // LANES
    for segment in range(message.shape[0]):
        partial = segment_of(sums, segment, per).astype(BF16)
        both = jnp.concatenate([own, partial], axis=0)
        message[segment] = jnp.concatenate([both, beside], axis=1)


def whiten(rows, cols, tiles, got, rest, n_col):
    n_row = got.shape[0]
    sub = rest.shape[1]
    return pl.pallas_call(
        whiten_kernel,
        out_shape=jax.ShapeDtypeStruct((n_col, 2 * NV, sub + LANES), BF16),
        in_specs=[SMEM, SMEM, VMEM, VMEM, VMEM],
        out_specs=VMEM,
        scratch_shapes=[pair_scratch(n_row, sub), pair_scratch(n_col, sub)],
        compiler_params=PARAMS,
        name="whiten_tiles",
    )(rows, cols, tiles, got, rest)


def joined(held):
    width = 4 * NV
    return held[:, :width] + held[:, width : 2 * width] + held[:, 2 * width : 3 * width]


def settle_kernel(
    total, rows, cols, tiles, moved, before, owned_before, rest, current,
    back, owned, following, upper_out, alphas, across_pairs, sums,
):
    n_col = moved.shape[0]
    sub = rest.shape[1]
    summed = jnp.zeros((NV, LANES), F32)
    for segment in range(n_col):
        summed = summed + moved[segment, :NV, sub:].astype(F32)
    alpha, upper, inverse = factor_of_sums(joined(summed) / total)
    upper_out[...] = upper
    alphas[...] = jnp.zeros_like(alphas)
    alphas[0] = alpha
    turn = dot_t(inverse, alpha)
    following[...] = dot(inverse, rest[...] - dot_tn(alpha, current[...]))

    def settle(segment, gathered):
        held = moved[segment].astype(F32)
        past = before[segment].astype(F32)[:NV]
        lower = joined(held[NV:, sub:])[:, :NV]
        change = mix(inverse, lower)
        put_pairs(mix(change, held[:NV, :sub]) - mix(turn, past), segment, across_pairs)
        return gathered + mix(change, held[NV:, :sub])

    gathered = lax.fori_loop(0, n_col, settle, jnp.zeros((NV, sub), F32), unroll=4)
    owned[...] = gathered - mix(turn, owned_before[...])
    end_pairs(across_pairs)
    accumulate(rows, cols, tiles, across_pairs, sums, BEHIND, split=2)
    per = sub // LANES
    for segment in range(back.shape[0]):
        back[segment] = segment_of(sums, segment, per)


def settle(rows, cols, tiles, moved, before, owned_before, rest, current, total, n_row):
    n_col = moved.shape[0]
    sub = rest.shape[1]
    return pl.pallas_call(
        functools.partial(settle_kernel, total),
        out_shape=(
            jax.ShapeDtypeStruct((n_row, NV, sub), F32),
            jax.ShapeDtypeStruct((NV, sub), F32),
            jax.ShapeDtypeStruct((NV, sub), F32),
            jax.ShapeDtypeStruct((NV, NV), F32),
            jax.ShapeDtypeStruct((STEPS, NV, NV), F32),
        ),
        in_specs=[SMEM, SMEM] + [VMEM] * 6,
        out_specs=(VMEM,) * 5,
        scratch_shapes=[pair_scratch(n_col, sub), pair_scratch(n_row, sub)],
        compiler_params=PARAMS,
        name="settle_tiles",
    )(rows, cols, tiles, moved, before, owned_before, rest, current)


def spread_kernel(parts, sums):
    one = jnp.sum(parts[...], axis=0)
    sums[...] = jnp.broadcast_to(one[None], sums.shape)


def spread(parts, copies):
    return pl.pallas_call(
        spread_kernel,
        out_shape=jax.ShapeDtypeStruct((copies, 2, LANES), F32),
        in_specs=[VMEM],
        out_specs=VMEM,
        compiler_params=PARAMS,
        name="spread_sums",
    )(parts)


def last_kernel(total, parts, rest, current, found, alphas, following):
    packed = jnp.sum(parts[...], axis=0) / total
    width = LANES // 4
    summed = jnp.concatenate(
        [packed[v // 4 : v // 4 + 1, v % 4 * width : (v % 4 + 1) * width] for v in range(NV)],
        axis=0,
    )
    alpha, _, inverse = factor_of_sums(summed)
    alphas[...] = found[...]
    alphas[STEPS - 1] = alpha
    following[...] = dot(inverse, rest[...] - dot_tn(alpha, current[...]))


def last(parts, rest, current, found, total):
    return pl.pallas_call(
        functools.partial(last_kernel, total),
        out_shape=(
            jax.ShapeDtypeStruct(found.shape, F32),
            jax.ShapeDtypeStruct(current.shape, F32),
        ),
        in_specs=[VMEM] * 4,
        out_specs=(VMEM, VMEM),
        compiler_params=PARAMS,
        name="last_block",
    )(parts, rest, current, found)


def swap(blocks, axis, groups=None):
    return lax.all_to_all(blocks, axis, 0, 0, tiled=True, axis_index_groups=groups)


def planes_and_lines(n_row, n_col):
    depth = DEPTH if n_col % DEPTH == 0 else n_col
    lines = [
        [row * n_col + high * depth + z for z in range(depth)]
        for row in range(n_row)
        for high in range(n_col // depth)
    ]
    planes = [[line[z] for line in lines] for z in range(depth)]
    return planes, lines


def shards(tiles, tile_row, tile_col, tile_count, block, previous, coupling):
    slots = tiles.shape[0]
    sub = block.shape[1]
    n_row = lax.axis_size("row")
    n_col = lax.axis_size("col")
    total = float(sub * n_row * n_col)
    squares = tiles.reshape(slots, TILE, TILE)
    live = lax.iota(jnp.int32, slots) < tile_count[0]
    rows = jnp.where(live, tile_row, n_col * sub // TILE)
    cols = jnp.where(live, tile_col, n_row * sub // TILE)
    planes, lines = planes_and_lines(n_row, n_col)
    narrow = block.astype(BF16)

    band = swap(jnp.broadcast_to(narrow[None], (n_row, NV, sub)), "row")
    before = swap(front(rows, cols, squares, band, narrow, n_col), "col")
    partial, owned = back(rows, cols, squares, before, n_row)
    returned = swap(partial, "row")
    rest, message = carry(owned, returned, block, previous, coupling, n_row)

    got = swap(message, "row")
    moved = swap(whiten(rows, cols, squares, got, rest, n_col), "col")
    partial, owned, current, upper, found = settle(
        rows, cols, squares, moved, before, owned, rest, block, total, n_row
    )
    returned = swap(partial, "row")
    rest, sums = local(owned, returned, current, block, upper, len(planes[0]))
    sums = spread(swap(sums, BOTH, planes), len(lines[0]))
    parts = swap(sums, BOTH, lines)
    found, current = last(parts, rest, current, found, total)
    return (current, found)


def solution(mesh):
    in_specs = (
        P(("row", "col"), None),
        P(("row", "col")),
        P(("row", "col")),
        P(("row", "col")),
        P(None, ("row", "col")),
        P(None, ("row", "col")),
        P(),
    )
    out_specs = (P(None, ("row", "col")), P())
    return jax.shard_map(shards, mesh=mesh, in_specs=in_specs, out_specs=out_specs, check_vma=False)
```

```python
import functools

import jax
import jax.numpy as jnp
from jax import lax
from jax.experimental import pallas as pl
from jax.experimental.pallas import tpu as pltpu
from jax.sharding import PartitionSpec as P

TILE = 64
NV = 8
STEPS = 2
LANES = 128
GROUP = 32
AHEAD = (((1,), (1,)), ((), ()))
BEHIND = (((1,), (0,)), ((), ()))
HIGH = lax.Precision.HIGHEST
F32 = jnp.float32
BF16 = jnp.bfloat16
VMEM = pl.BlockSpec(memory_space=pltpu.VMEM)
SMEM = pl.BlockSpec(memory_space=pltpu.SMEM)
PARAMS = pltpu.CompilerParams(vmem_limit_bytes=40 * 1024 * 1024)


def dot(left, right):
    return jnp.dot(left, right, precision=HIGH, preferred_element_type=F32)


def dot_t(left, right):
    return lax.dot_general(
        left, right, (((1,), (1,)), ((), ())), precision=HIGH, preferred_element_type=F32
    )


def dot_tn(left, right):
    return lax.dot_general(
        left, right, (((0,), (0,)), ((), ())), precision=HIGH, preferred_element_type=F32
    )


def lane_half():
    return lax.broadcasted_iota(jnp.int32, (NV, LANES), 1) // TILE


def narrowed(pair, mask):
    held = jnp.where(mask, pair, 0.0)
    return (held + pltpu.roll(held, TILE, 1))[:, :TILE]


def pieces(value, count):
    found = []
    for _ in range(count):
        piece = value.astype(BF16)
        value = value - piece.astype(F32)
        found.append(piece)
    return found


def product_of(picked, tile, dims, split):
    if split == 1:
        return lax.dot_general(picked.astype(BF16), tile, dims, preferred_element_type=F32)
    both = jnp.concatenate(pieces(picked, 2), axis=0)
    out = lax.dot_general(both, tile, dims, preferred_element_type=F32)
    return out[:NV] + out[NV:]


def both_halves(product, mask):
    return jnp.where(mask, jnp.concatenate([product, product], axis=1), 0.0)


def mix(coefficients, rows):
    out = coefficients[:, 0:1] * rows[0:1]
    for v in range(1, NV):
        out = out + coefficients[:, v : v + 1] * rows[v : v + 1]
    return out


def factor(gram):
    row = lax.broadcasted_iota(jnp.int32, (NV, 2 * NV), 0)
    lane = lax.broadcasted_iota(jnp.int32, (NV, 2 * NV), 1)
    unit = jnp.where(row + NV == lane, 1.0, 0.0).astype(F32)
    work = jnp.concatenate([gram, unit[:, NV:]], axis=1)
    for j in range(NV):
        pivot = jnp.sqrt(work[j : j + 1, j : j + 1])
        scaled = work[j : j + 1, :] / pivot
        column = work[:, j : j + 1] / pivot
        work = jnp.where(row == j, scaled, jnp.where(row > j, work - column * scaled, work))
    return jnp.where(row <= lane, work, 0.0)[:, :NV], work[:, NV:]


def factor_of_sums(summed):
    alpha = summed[:, :NV]
    mixed = summed[:, NV : 2 * NV]
    own = summed[:, 2 * NV : 3 * NV]
    square = summed[:, 3 * NV : 4 * NV]
    gram = square - dot_tn(alpha, mixed) - dot_tn(mixed, alpha) + dot_tn(alpha, dot(own, alpha))
    return (alpha, *factor(gram))


def identity():
    row = lax.broadcasted_iota(jnp.int32, (NV, NV), 0)
    lane = lax.broadcasted_iota(jnp.int32, (NV, NV), 1)
    return jnp.where(row == lane, 1.0, 0.0).astype(F32)


def put_pairs(held, segment, pairs):
    per = held.shape[1] // LANES
    for part in range(per):
        pairs[segment * per + part] = held[:, part * LANES : (part + 1) * LANES]


def end_pairs(pairs):
    pairs[pairs.shape[0] - 1] = jnp.zeros((NV, LANES), F32)


def to_pairs(segments, pairs):
    for segment in range(segments.shape[0]):
        put_pairs(segments[segment].astype(F32), segment, pairs)
    end_pairs(pairs)


def part_rows(part):
    return pl.ds(part * 2 * NV, 2 * NV)


def put_message(message, own, sums, per):
    for segment in range(message.shape[0]):
        for part in range(per):
            mine = own[:, part * LANES : (part + 1) * LANES]
            partial = sums[segment * per + part].astype(BF16)
            message[segment, part_rows(part)] = jnp.concatenate([mine, partial], axis=0)


def segment_of(pairs, segment, per):
    parts = [pairs[segment * per + part] for part in range(per)]
    return jnp.concatenate(parts, axis=1)


def pair_scratch(count, sub):
    return pltpu.VMEM((count * sub // LANES + 1, NV, LANES), F32)


def accumulate(reads, writes, tiles, pairs, sums, dims, split=1):
    half = lane_half()
    sums[...] = jnp.zeros_like(sums)

    def group(g, carry):
        updates = []
        for u in range(GROUP):
            k = g * GROUP + u
            read, write = reads[k], writes[k]
            picked = narrowed(pairs[lax.shift_right_logical(read, 1)], half == (read & 1))
            out = both_halves(product_of(picked, tiles[k], dims, split), half == (write & 1))
            updates.append((lax.shift_right_logical(write, 1), out))
        for pair, out in updates:
            sums[pair] += out
        return carry

    lax.fori_loop(0, tiles.shape[0] // GROUP, group, 0)


def front_kernel(rows, cols, tiles, band, narrow, message, band_pairs, sums):
    to_pairs(band, band_pairs)
    accumulate(cols, rows, tiles, band_pairs, sums, AHEAD)
    put_message(message, narrow[...], sums, band.shape[2] // LANES)


def front(rows, cols, tiles, band, narrow, n_col):
    n_row, _, sub = band.shape
    return pl.pallas_call(
        front_kernel,
        out_shape=jax.ShapeDtypeStruct((n_col, 2 * NV * sub // LANES, LANES), BF16),
        in_specs=[SMEM, SMEM, VMEM, VMEM, VMEM],
        out_specs=VMEM,
        scratch_shapes=[pair_scratch(n_row, sub), pair_scratch(n_col, sub)],
        compiler_params=PARAMS,
        name="front_tiles",
    )(rows, cols, tiles, band, narrow)


def back_kernel(rows, cols, tiles, moved, back, owned, across_pairs, sums):
    per = back.shape[2] // LANES
    gathered = []
    for part in range(per):
        total = jnp.zeros((NV, LANES), F32)
        for segment in range(moved.shape[0]):
            held = moved[segment, part_rows(part)].astype(F32)
            across_pairs[segment * per + part] = held[:NV]
            total = total + held[NV:]
        gathered.append(total)
    end_pairs(across_pairs)
    owned[...] = jnp.concatenate(gathered, axis=1)
    accumulate(rows, cols, tiles, across_pairs, sums, BEHIND)
    for segment in range(back.shape[0]):
        back[segment] = segment_of(sums, segment, per)


def back(rows, cols, tiles, moved, n_row, sub):
    n_col = moved.shape[0]
    return pl.pallas_call(
        back_kernel,
        out_shape=(
            jax.ShapeDtypeStruct((n_row, NV, sub), F32),
            jax.ShapeDtypeStruct((NV, sub), F32),
        ),
        in_specs=[SMEM, SMEM, VMEM, VMEM],
        out_specs=(VMEM, VMEM),
        scratch_shapes=[pair_scratch(n_col, sub), pair_scratch(n_row, sub)],
        compiler_params=PARAMS,
        name="back_tiles",
    )(rows, cols, tiles, moved)


def rest_and_sums(owned, returned, current, prior, beta):
    image = owned[...] + jnp.sum(returned[...], axis=0)
    now = current[...]
    rest = image - dot(beta[...], prior[...])
    left = jnp.concatenate([now, rest], axis=0)
    right = jnp.concatenate([image, rest, now], axis=0)
    inner = dot_t(left, right)
    return rest, jnp.concatenate([inner[:NV], inner[NV:, NV : 2 * NV]], axis=1)


def local_kernel(owned, returned, current, prior, beta, ahead, sums):
    rest, blocks = rest_and_sums(owned, returned, current, prior, beta)
    ahead[...] = rest
    packed = [
        jnp.concatenate([blocks[v : v + 1] for v in range(part, part + 4)], axis=1)
        for part in (0, 4)
    ]
    one = jnp.concatenate(packed, axis=0)
    sums[...] = jnp.broadcast_to(one[None], sums.shape)


def local(owned, returned, current, prior, beta, copies):
    return pl.pallas_call(
        local_kernel,
        out_shape=(
            jax.ShapeDtypeStruct(current.shape, F32),
            jax.ShapeDtypeStruct((copies, 2, LANES), F32),
        ),
        in_specs=[VMEM] * 5,
        out_specs=(VMEM, VMEM),
        compiler_params=PARAMS,
        name="local_sums",
    )(owned, returned, current, prior, beta)


def carry_kernel(owned, returned, current, prior, beta, ahead, message):
    rest, blocks = rest_and_sums(owned, returned, current, prior, beta)
    ahead[...] = rest
    pad = jnp.zeros((NV, LANES - 4 * NV), F32)
    one = jnp.concatenate([rest, blocks, pad], axis=1)
    message[...] = jnp.broadcast_to(one[None], message.shape)


def carry(owned, returned, current, prior, beta, n_row):
    sub = current.shape[1]
    return pl.pallas_call(
        carry_kernel,
        out_shape=(
            jax.ShapeDtypeStruct(current.shape, F32),
            jax.ShapeDtypeStruct((n_row, NV, sub + LANES), F32),
        ),
        in_specs=[VMEM] * 5,
        out_specs=(VMEM, VMEM),
        compiler_params=PARAMS,
        name="local_carry",
    )(owned, returned, current, prior, beta)


def whiten_kernel(rows, cols, tiles, got, rest, message, band_pairs, sums):
    n_row = got.shape[0]
    sub = rest.shape[1]
    summed = jnp.sum(got[:, :, sub:], axis=0)[:, : 4 * NV]
    gram = summed[:, 3 * NV :] / float(n_row * sub)
    unit = identity()
    trace = jnp.sum(jnp.sum(gram * unit, axis=1, keepdims=True), axis=0, keepdims=True)
    upper, inverse = factor(gram + (trace * 1e-5 + 1e-30) * unit)
    lower = dot_tn(upper, unit)
    for segment in range(n_row):
        put_pairs(mix(inverse, got[segment, :, :sub]), segment, band_pairs)
    end_pairs(band_pairs)
    own = mix(inverse, rest[...]).astype(BF16)
    twice = jnp.concatenate([lower, lower], axis=1)
    beside = jnp.concatenate(pieces(summed, 3) + pieces(twice, 2), axis=1)
    accumulate(cols, rows, tiles, band_pairs, sums, AHEAD)
    per = sub // LANES
    put_message(message, own, sums, per)
    for segment in range(message.shape[0]):
        message[segment, pl.ds(2 * NV * per, NV)] = beside


def whiten(rows, cols, tiles, got, rest, n_col):
    n_row = got.shape[0]
    sub = rest.shape[1]
    return pl.pallas_call(
        whiten_kernel,
        out_shape=jax.ShapeDtypeStruct((n_col, 2 * NV * sub // LANES + NV, LANES), BF16),
        in_specs=[SMEM, SMEM, VMEM, VMEM, VMEM],
        out_specs=VMEM,
        scratch_shapes=[pair_scratch(n_row, sub), pair_scratch(n_col, sub)],
        compiler_params=PARAMS,
        name="whiten_tiles",
    )(rows, cols, tiles, got, rest)


def joined(held):
    width = 4 * NV
    return held[:, :width] + held[:, width : 2 * width] + held[:, 2 * width : 3 * width]


def settle_kernel(
    total, rows, cols, tiles, moved, before, rest, current,
    back, owned, following, upper_out, alphas, across_pairs, sums,
):
    n_col = moved.shape[0]
    sub = rest.shape[1]
    per = sub // LANES
    beside = pl.ds(2 * NV * per, NV)
    summed = jnp.zeros((NV, LANES), F32)
    for segment in range(n_col):
        summed = summed + moved[segment, beside].astype(F32)
    alpha, upper, inverse = factor_of_sums(joined(summed) / total)
    upper_out[...] = upper
    alphas[...] = jnp.zeros_like(alphas)
    alphas[0] = alpha
    turn = -dot_t(inverse, alpha)
    following[...] = dot(inverse, rest[...] - dot_tn(alpha, current[...]))
    columns = [jnp.broadcast_to(inverse[:, v : v + 1], (NV, LANES)) for v in range(NV)]
    four = 4 * NV
    lane = lax.broadcasted_iota(jnp.int32, (NV, four), 1)
    segment_lanes = (lane & NV) == 0
    turns = jnp.concatenate([turn] * 4, axis=1)

    def settle(segment, gathered):
        held = moved[segment, beside].astype(F32)
        held = held + pltpu.roll(held, 2 * NV, 1)
        change = columns[0] * held[0:1]
        for v in range(1, NV):
            change = change + columns[v] * held[v : v + 1]
        change = pltpu.roll(change, 2 * NV, 1)[:, :four]
        change = jnp.where(lane < 2 * NV, change, turns)
        high = change.astype(BF16).astype(F32)
        both = jnp.concatenate([high, change - high], axis=0)
        mask = jnp.concatenate([segment_lanes, segment_lanes], axis=0)
        left = jnp.concatenate([jnp.where(mask, both, 0.0), jnp.where(mask, 0.0, both)], axis=0)
        parts = []
        for part in range(per):
            now = moved[segment, part_rows(part)]
            past = before[segment, part_rows(part)]
            parts.append(jnp.concatenate([now, past], axis=0))
        right = jnp.concatenate(parts, axis=1)
        out = jnp.dot(left.astype(BF16), right, preferred_element_type=F32)
        put_pairs(out[:NV] + out[NV : 2 * NV], segment, across_pairs)
        return gathered + (out[2 * NV : 3 * NV] + out[3 * NV :])

    owned[...] = lax.fori_loop(0, n_col, settle, jnp.zeros((NV, sub), F32), unroll=8)
    end_pairs(across_pairs)
    accumulate(rows, cols, tiles, across_pairs, sums, BEHIND, split=2)
    for segment in range(back.shape[0]):
        back[segment] = segment_of(sums, segment, per)


def settle(rows, cols, tiles, moved, before, rest, current, total, n_row):
    n_col = moved.shape[0]
    sub = rest.shape[1]
    return pl.pallas_call(
        functools.partial(settle_kernel, total),
        out_shape=(
            jax.ShapeDtypeStruct((n_row, NV, sub), F32),
            jax.ShapeDtypeStruct((NV, sub), F32),
            jax.ShapeDtypeStruct((NV, sub), F32),
            jax.ShapeDtypeStruct((NV, NV), F32),
            jax.ShapeDtypeStruct((STEPS, NV, NV), F32),
        ),
        in_specs=[SMEM, SMEM] + [VMEM] * 5,
        out_specs=(VMEM,) * 5,
        scratch_shapes=[pair_scratch(n_col, sub), pair_scratch(n_row, sub)],
        compiler_params=PARAMS,
        name="settle_tiles",
    )(rows, cols, tiles, moved, before, rest, current)


def spread_kernel(parts, sums):
    one = jnp.sum(parts[...], axis=0)
    sums[...] = jnp.broadcast_to(one[None], sums.shape)


def spread(parts, copies):
    return pl.pallas_call(
        spread_kernel,
        out_shape=jax.ShapeDtypeStruct((copies, 2, LANES), F32),
        in_specs=[VMEM],
        out_specs=VMEM,
        compiler_params=PARAMS,
        name="spread_sums",
    )(parts)


def last_kernel(total, parts, rest, current, found, alphas, following):
    packed = jnp.sum(parts[...], axis=0) / total
    width = LANES // 4
    summed = jnp.concatenate(
        [packed[v // 4 : v // 4 + 1, v % 4 * width : (v % 4 + 1) * width] for v in range(NV)],
        axis=0,
    )
    alpha, _, inverse = factor_of_sums(summed)
    alphas[...] = found[...]
    alphas[STEPS - 1] = alpha
    following[...] = dot(inverse, rest[...] - dot_tn(alpha, current[...]))


def last(parts, rest, current, found, total):
    return pl.pallas_call(
        functools.partial(last_kernel, total),
        out_shape=(
            jax.ShapeDtypeStruct(found.shape, F32),
            jax.ShapeDtypeStruct(current.shape, F32),
        ),
        in_specs=[VMEM] * 4,
        out_specs=(VMEM, VMEM),
        compiler_params=PARAMS,
        name="last_block",
    )(parts, rest, current, found)


def round_kernel(block, narrow, copies):
    held = block[...].astype(BF16)
    narrow[...] = held
    copies[...] = jnp.broadcast_to(held[None], copies.shape)


def round_block(block, n_row):
    return pl.pallas_call(
        round_kernel,
        out_shape=(
            jax.ShapeDtypeStruct(block.shape, BF16),
            jax.ShapeDtypeStruct((n_row, *block.shape), BF16),
        ),
        in_specs=[VMEM],
        out_specs=(VMEM, VMEM),
        compiler_params=PARAMS,
        name="round_block",
    )(block)


def swap(blocks, axis):
    return lax.all_to_all(blocks, axis, 0, 0, tiled=True)


def shards(tiles, tile_row, tile_col, tile_count, block, previous, coupling):
    slots = tiles.shape[0]
    sub = block.shape[1]
    n_row = lax.axis_size("row")
    n_col = lax.axis_size("col")
    total = float(sub * n_row * n_col)
    squares = tiles.reshape(slots, TILE, TILE)
    live = lax.iota(jnp.int32, slots) < tile_count[0]
    rows = jnp.where(live, tile_row, n_col * sub // TILE)
    cols = jnp.where(live, tile_col, n_row * sub // TILE)
    narrow, copies = round_block(block, n_row)

    band = swap(copies, "row")
    before = swap(front(rows, cols, squares, band, narrow, n_col), "col")
    partial, owned = back(rows, cols, squares, before, n_row, sub)
    returned = swap(partial, "row")
    rest, message = carry(owned, returned, block, previous, coupling, n_row)

    got = swap(message, "row")
    moved = swap(whiten(rows, cols, squares, got, rest, n_col), "col")
    partial, owned, current, upper, found = settle(
        rows, cols, squares, moved, before, rest, block, total, n_row
    )
    returned = swap(partial, "row")
    rest, sums = local(owned, returned, current, block, upper, n_row)
    parts = swap(spread(swap(sums, "row"), n_col), "col")
    found, current = last(parts, rest, current, found, total)
    return (current, found)


def solution(mesh):
    in_specs = (
        P(("row", "col"), None),
        P(("row", "col")),
        P(("row", "col")),
        P(("row", "col")),
        P(None, ("row", "col")),
        P(None, ("row", "col")),
        P(),
    )
    out_specs = (P(None, ("row", "col")), P())
    return jax.shard_map(shards, mesh=mesh, in_specs=in_specs, out_specs=out_specs, check_vma=False)
```

```python
import functools

import jax
import jax.numpy as jnp
from jax import lax
from jax.experimental import pallas as pl
from jax.experimental.pallas import tpu as pltpu
from jax.sharding import PartitionSpec as P

TILE = 64
NV = 8
STEPS = 2
LANES = 128
GROUP = 16
AHEAD = (((1,), (1,)), ((), ()))
BEHIND = (((1,), (0,)), ((), ()))
HIGH = lax.Precision.HIGHEST
F32 = jnp.float32
BF16 = jnp.bfloat16
VMEM = pl.BlockSpec(memory_space=pltpu.VMEM)
SMEM = pl.BlockSpec(memory_space=pltpu.SMEM)
PARAMS = pltpu.CompilerParams(vmem_limit_bytes=40 * 1024 * 1024)


def dot(left, right):
    return jnp.dot(left, right, precision=HIGH, preferred_element_type=F32)


def dot_t(left, right):
    return lax.dot_general(
        left, right, (((1,), (1,)), ((), ())), precision=HIGH, preferred_element_type=F32
    )


def dot_tn(left, right):
    return lax.dot_general(
        left, right, (((0,), (0,)), ((), ())), precision=HIGH, preferred_element_type=F32
    )


def lane_half():
    return lax.broadcasted_iota(jnp.int32, (NV, LANES), 1) // TILE


def narrowed(pair, mask):
    held = jnp.where(mask, pair, 0.0)
    return (held + pltpu.roll(held, TILE, 1))[:, :TILE]


def pieces(value, count):
    found = []
    for _ in range(count):
        piece = value.astype(BF16)
        value = value - piece.astype(F32)
        found.append(piece)
    return found


def product_of(picked, tile, dims, split):
    if split == 1:
        return lax.dot_general(picked.astype(BF16), tile, dims, preferred_element_type=F32)
    both = jnp.concatenate(pieces(picked, 2), axis=0)
    out = lax.dot_general(both, tile, dims, preferred_element_type=F32)
    return out[:NV] + out[NV:]


def both_halves(product, mask):
    return jnp.where(mask, jnp.concatenate([product, product], axis=1), 0.0)


def mix(coefficients, rows):
    out = coefficients[:, 0:1] * rows[0:1]
    for v in range(1, NV):
        out = out + coefficients[:, v : v + 1] * rows[v : v + 1]
    return out


def factor(gram):
    row = lax.broadcasted_iota(jnp.int32, (NV, 2 * NV), 0)
    lane = lax.broadcasted_iota(jnp.int32, (NV, 2 * NV), 1)
    unit = jnp.where(row + NV == lane, 1.0, 0.0).astype(F32)
    work = jnp.concatenate([gram, unit[:, NV:]], axis=1)
    for j in range(NV):
        scale = 1.0 / jnp.sqrt(work[j : j + 1, j : j + 1])
        scaled = work[j : j + 1, :] * scale
        column = work[:, j : j + 1] * scale
        work = jnp.where(row == j, scaled, jnp.where(row > j, work - column * scaled, work))
    return jnp.where(row <= lane, work, 0.0)[:, :NV], work[:, NV:]


def factor_of_sums(summed):
    alpha = summed[:, :NV]
    mixed = summed[:, NV : 2 * NV]
    own = summed[:, 2 * NV : 3 * NV]
    square = summed[:, 3 * NV : 4 * NV]
    gram = square - dot_tn(alpha, mixed) - dot_tn(mixed, alpha) + dot_tn(alpha, dot(own, alpha))
    return (alpha, *factor(gram))


def identity():
    row = lax.broadcasted_iota(jnp.int32, (NV, NV), 0)
    lane = lax.broadcasted_iota(jnp.int32, (NV, NV), 1)
    return jnp.where(row == lane, 1.0, 0.0).astype(F32)


def put_pairs(held, segment, pairs):
    per = held.shape[1] // LANES
    for part in range(per):
        pairs[segment * per + part] = held[:, part * LANES : (part + 1) * LANES]


def end_pairs(pairs):
    pairs[pairs.shape[0] - 1] = jnp.zeros((NV, LANES), F32)


def to_pairs(segments, pairs):
    for segment in range(segments.shape[0]):
        put_pairs(segments[segment].astype(F32), segment, pairs)
    end_pairs(pairs)


def part_rows(part):
    return pl.ds(part * 2 * NV, 2 * NV)


def put_message(message, own, sums, per):
    for segment in range(message.shape[0]):
        for part in range(per):
            mine = own[:, part * LANES : (part + 1) * LANES]
            partial = sums[segment * per + part].astype(BF16)
            message[segment, part_rows(part)] = jnp.concatenate([mine, partial], axis=0)


def segment_of(pairs, segment, per):
    parts = [pairs[segment * per + part] for part in range(per)]
    return jnp.concatenate(parts, axis=1)


def pair_scratch(count, sub):
    return pltpu.VMEM((count * sub // LANES + 1, NV, LANES), F32)


def accumulate(reads, writes, tiles, pairs, sums, dims, split=1):
    half = lane_half()
    sums[...] = jnp.zeros_like(sums)

    slots = tiles.shape[0]
    for first in range(0, slots, GROUP):
        updates = []
        for k in range(first, min(first + GROUP, slots)):
            read, write = reads[k], writes[k]
            picked = narrowed(pairs[lax.shift_right_logical(read, 1)], half == (read & 1))
            out = both_halves(product_of(picked, tiles[k], dims, split), half == (write & 1))
            updates.append((lax.shift_right_logical(write, 1), out))
        for pair, out in updates:
            sums[pair] += out


def front_kernel(rows, cols, tiles, band, narrow, message, band_pairs, sums):
    to_pairs(band, band_pairs)
    accumulate(cols, rows, tiles, band_pairs, sums, AHEAD)
    put_message(message, narrow[...], sums, band.shape[2] // LANES)


def front(rows, cols, tiles, band, narrow, n_col):
    n_row, _, sub = band.shape
    return pl.pallas_call(
        front_kernel,
        out_shape=jax.ShapeDtypeStruct((n_col, 2 * NV * sub // LANES, LANES), BF16),
        in_specs=[SMEM, SMEM, VMEM, VMEM, VMEM],
        out_specs=VMEM,
        scratch_shapes=[pair_scratch(n_row, sub), pair_scratch(n_col, sub)],
        compiler_params=PARAMS,
        name="front_tiles",
    )(rows, cols, tiles, band, narrow)


def back_kernel(rows, cols, tiles, moved, back, owned, across_pairs, sums):
    per = back.shape[2] // LANES
    gathered = []
    for part in range(per):
        total = jnp.zeros((NV, LANES), F32)
        for segment in range(moved.shape[0]):
            held = moved[segment, part_rows(part)].astype(F32)
            across_pairs[segment * per + part] = held[:NV]
            total = total + held[NV:]
        gathered.append(total)
    end_pairs(across_pairs)
    owned[...] = jnp.concatenate(gathered, axis=1)
    accumulate(rows, cols, tiles, across_pairs, sums, BEHIND)
    for segment in range(back.shape[0]):
        back[segment] = segment_of(sums, segment, per)


def back(rows, cols, tiles, moved, n_row, sub):
    n_col = moved.shape[0]
    return pl.pallas_call(
        back_kernel,
        out_shape=(
            jax.ShapeDtypeStruct((n_row, NV, sub), F32),
            jax.ShapeDtypeStruct((NV, sub), F32),
        ),
        in_specs=[SMEM, SMEM, VMEM, VMEM],
        out_specs=(VMEM, VMEM),
        scratch_shapes=[pair_scratch(n_col, sub), pair_scratch(n_row, sub)],
        compiler_params=PARAMS,
        name="back_tiles",
    )(rows, cols, tiles, moved)


def rest_and_sums(owned, returned, current, prior, beta):
    image = owned[...] + jnp.sum(returned[...], axis=0)
    now = current[...]
    rest = image - dot(beta[...], prior[...])
    left = jnp.concatenate([now, rest], axis=0)
    right = jnp.concatenate([image, rest, now], axis=0)
    inner = dot_t(left, right)
    return rest, jnp.concatenate([inner[:NV], inner[NV:, NV : 2 * NV]], axis=1)


def local_kernel(owned, returned, current, prior, beta, ahead, sums):
    rest, blocks = rest_and_sums(owned, returned, current, prior, beta)
    ahead[...] = rest
    packed = [
        jnp.concatenate([blocks[v : v + 1] for v in range(part, part + 4)], axis=1)
        for part in (0, 4)
    ]
    one = jnp.concatenate(packed, axis=0)
    sums[...] = jnp.broadcast_to(one[None], sums.shape)


def local(owned, returned, current, prior, beta, copies):
    return pl.pallas_call(
        local_kernel,
        out_shape=(
            jax.ShapeDtypeStruct(current.shape, F32),
            jax.ShapeDtypeStruct((copies, 2, LANES), F32),
        ),
        in_specs=[VMEM] * 5,
        out_specs=(VMEM, VMEM),
        compiler_params=PARAMS,
        name="local_sums",
    )(owned, returned, current, prior, beta)


def carry_kernel(owned, returned, current, prior, beta, ahead, message):
    rest, blocks = rest_and_sums(owned, returned, current, prior, beta)
    ahead[...] = rest
    pad = jnp.zeros((NV, LANES - 4 * NV), F32)
    one = jnp.concatenate([rest, blocks, pad], axis=1)
    message[...] = jnp.broadcast_to(one[None], message.shape)


def carry(owned, returned, current, prior, beta, n_row):
    sub = current.shape[1]
    return pl.pallas_call(
        carry_kernel,
        out_shape=(
            jax.ShapeDtypeStruct(current.shape, F32),
            jax.ShapeDtypeStruct((n_row, NV, sub + LANES), F32),
        ),
        in_specs=[VMEM] * 5,
        out_specs=(VMEM, VMEM),
        compiler_params=PARAMS,
        name="local_carry",
    )(owned, returned, current, prior, beta)


def whiten_kernel(rows, cols, tiles, got, rest, message, band_pairs, sums):
    n_row = got.shape[0]
    sub = rest.shape[1]
    summed = jnp.sum(got[:, :, sub:], axis=0)[:, : 4 * NV]
    gram = summed[:, 3 * NV :] / float(n_row * sub)
    unit = identity()
    trace = jnp.sum(jnp.sum(gram * unit, axis=1, keepdims=True), axis=0, keepdims=True)
    upper, inverse = factor(gram + (trace * 1e-5 + 1e-30) * unit)
    lower = dot_tn(upper, unit)
    for segment in range(n_row):
        put_pairs(mix(inverse, got[segment, :, :sub]), segment, band_pairs)
    end_pairs(band_pairs)
    own = mix(inverse, rest[...]).astype(BF16)
    twice = jnp.concatenate([lower, lower], axis=1)
    beside = jnp.concatenate(pieces(summed, 3) + pieces(twice, 2), axis=1)
    accumulate(cols, rows, tiles, band_pairs, sums, AHEAD)
    per = sub // LANES
    put_message(message, own, sums, per)
    for segment in range(message.shape[0]):
        message[segment, pl.ds(2 * NV * per, NV)] = beside


def whiten(rows, cols, tiles, got, rest, n_col):
    n_row = got.shape[0]
    sub = rest.shape[1]
    return pl.pallas_call(
        whiten_kernel,
        out_shape=jax.ShapeDtypeStruct((n_col, 2 * NV * sub // LANES + NV, LANES), BF16),
        in_specs=[SMEM, SMEM, VMEM, VMEM, VMEM],
        out_specs=VMEM,
        scratch_shapes=[pair_scratch(n_row, sub), pair_scratch(n_col, sub)],
        compiler_params=PARAMS,
        name="whiten_tiles",
    )(rows, cols, tiles, got, rest)


def joined(held):
    width = 4 * NV
    return held[:, :width] + held[:, width : 2 * width] + held[:, 2 * width : 3 * width]


def settle_kernel(
    total, rows, cols, tiles, moved, before, rest, current,
    back, owned, following, upper_out, alphas, across_pairs, sums,
):
    n_col = moved.shape[0]
    sub = rest.shape[1]
    per = sub // LANES
    beside = pl.ds(2 * NV * per, NV)
    summed = jnp.zeros((NV, LANES), F32)
    for segment in range(n_col):
        summed = summed + moved[segment, beside].astype(F32)
    alpha, upper, inverse = factor_of_sums(joined(summed) / total)
    upper_out[...] = upper
    alphas[...] = jnp.zeros_like(alphas)
    alphas[0] = alpha
    turn = -dot_t(inverse, alpha)
    following[...] = dot(inverse, rest[...] - dot_tn(alpha, current[...]))
    columns = [jnp.broadcast_to(inverse[:, v : v + 1], (NV, LANES)) for v in range(NV)]
    four = 4 * NV
    lane = lax.broadcasted_iota(jnp.int32, (NV, four), 1)
    segment_lanes = (lane & NV) == 0
    turns = jnp.concatenate([turn] * 4, axis=1)

    def settle(segment, gathered):
        held = moved[segment, beside].astype(F32)
        held = held + pltpu.roll(held, 2 * NV, 1)
        change = columns[0] * held[0:1]
        for v in range(1, NV):
            change = change + columns[v] * held[v : v + 1]
        change = pltpu.roll(change, 2 * NV, 1)[:, :four]
        change = jnp.where(lane < 2 * NV, change, turns)
        high = change.astype(BF16).astype(F32)
        both = jnp.concatenate([high, change - high], axis=0)
        mask = jnp.concatenate([segment_lanes, segment_lanes], axis=0)
        left = jnp.concatenate([jnp.where(mask, both, 0.0), jnp.where(mask, 0.0, both)], axis=0)
        parts = []
        for part in range(per):
            now = moved[segment, part_rows(part)]
            past = before[segment, part_rows(part)]
            parts.append(jnp.concatenate([now, past], axis=0))
        right = jnp.concatenate(parts, axis=1)
        out = jnp.dot(left.astype(BF16), right, preferred_element_type=F32)
        put_pairs(out[:NV] + out[NV : 2 * NV], segment, across_pairs)
        return gathered + (out[2 * NV : 3 * NV] + out[3 * NV :])

    owned[...] = lax.fori_loop(0, n_col, settle, jnp.zeros((NV, sub), F32), unroll=True)
    end_pairs(across_pairs)
    accumulate(rows, cols, tiles, across_pairs, sums, BEHIND, split=2)
    for segment in range(back.shape[0]):
        back[segment] = segment_of(sums, segment, per)


def settle(rows, cols, tiles, moved, before, rest, current, total, n_row):
    n_col = moved.shape[0]
    sub = rest.shape[1]
    return pl.pallas_call(
        functools.partial(settle_kernel, total),
        out_shape=(
            jax.ShapeDtypeStruct((n_row, NV, sub), F32),
            jax.ShapeDtypeStruct((NV, sub), F32),
            jax.ShapeDtypeStruct((NV, sub), F32),
            jax.ShapeDtypeStruct((NV, NV), F32),
            jax.ShapeDtypeStruct((STEPS, NV, NV), F32),
        ),
        in_specs=[SMEM, SMEM] + [VMEM] * 5,
        out_specs=(VMEM,) * 5,
        scratch_shapes=[pair_scratch(n_col, sub), pair_scratch(n_row, sub)],
        compiler_params=PARAMS,
        name="settle_tiles",
    )(rows, cols, tiles, moved, before, rest, current)


def spread_kernel(parts, sums):
    one = jnp.sum(parts[...], axis=0)
    sums[...] = jnp.broadcast_to(one[None], sums.shape)


def spread(parts, copies):
    return pl.pallas_call(
        spread_kernel,
        out_shape=jax.ShapeDtypeStruct((copies, 2, LANES), F32),
        in_specs=[VMEM],
        out_specs=VMEM,
        compiler_params=PARAMS,
        name="spread_sums",
    )(parts)


def last_kernel(total, parts, rest, current, found, alphas, following):
    packed = jnp.sum(parts[...], axis=0) / total
    width = LANES // 4
    summed = jnp.concatenate(
        [packed[v // 4 : v // 4 + 1, v % 4 * width : (v % 4 + 1) * width] for v in range(NV)],
        axis=0,
    )
    alpha, _, inverse = factor_of_sums(summed)
    alphas[...] = found[...]
    alphas[STEPS - 1] = alpha
    following[...] = dot(inverse, rest[...] - dot_tn(alpha, current[...]))


def last(parts, rest, current, found, total):
    return pl.pallas_call(
        functools.partial(last_kernel, total),
        out_shape=(
            jax.ShapeDtypeStruct(found.shape, F32),
            jax.ShapeDtypeStruct(current.shape, F32),
        ),
        in_specs=[VMEM] * 4,
        out_specs=(VMEM, VMEM),
        compiler_params=PARAMS,
        name="last_block",
    )(parts, rest, current, found)


def round_kernel(block, narrow, copies):
    held = block[...].astype(BF16)
    narrow[...] = held
    copies[...] = jnp.broadcast_to(held[None], copies.shape)


def round_block(block, n_row):
    return pl.pallas_call(
        round_kernel,
        out_shape=(
            jax.ShapeDtypeStruct(block.shape, BF16),
            jax.ShapeDtypeStruct((n_row, *block.shape), BF16),
        ),
        in_specs=[VMEM],
        out_specs=(VMEM, VMEM),
        compiler_params=PARAMS,
        name="round_block",
    )(block)


def swap(blocks, axis):
    return lax.all_to_all(blocks, axis, 0, 0, tiled=True)


def shards(tiles, tile_row, tile_col, tile_count, block, previous, coupling):
    slots = tiles.shape[0]
    sub = block.shape[1]
    n_row = lax.axis_size("row")
    n_col = lax.axis_size("col")
    total = float(sub * n_row * n_col)
    squares = tiles.reshape(slots, TILE, TILE)
    live = lax.iota(jnp.int32, slots) < tile_count[0]
    rows = jnp.where(live, tile_row, n_col * sub // TILE)
    cols = jnp.where(live, tile_col, n_row * sub // TILE)
    narrow, copies = round_block(block, n_row)

    band = swap(copies, "row")
    before = swap(front(rows, cols, squares, band, narrow, n_col), "col")
    partial, owned = back(rows, cols, squares, before, n_row, sub)
    returned = swap(partial, "row")
    rest, message = carry(owned, returned, block, previous, coupling, n_row)

    got = swap(message, "row")
    moved = swap(whiten(rows, cols, squares, got, rest, n_col), "col")
    partial, owned, current, upper, found = settle(
        rows, cols, squares, moved, before, rest, block, total, n_row
    )
    returned = swap(partial, "row")
    rest, sums = local(owned, returned, current, block, upper, n_row)
    parts = swap(spread(swap(sums, "row"), n_col), "col")
    found, current = last(parts, rest, current, found, total)
    return (current, found)


def solution(mesh):
    in_specs = (
        P(("row", "col"), None),
        P(("row", "col")),
        P(("row", "col")),
        P(("row", "col")),
        P(None, ("row", "col")),
        P(None, ("row", "col")),
        P(),
    )
    out_specs = (P(None, ("row", "col")), P())
    return jax.shard_map(shards, mesh=mesh, in_specs=in_specs, out_specs=out_specs, check_vma=False)
```

```python
import functools

import jax
import jax.numpy as jnp
from jax import lax
from jax.experimental import pallas as pl
from jax.experimental.pallas import tpu as pltpu
from jax.sharding import PartitionSpec as P

TILE = 64
NV = 8
STEPS = 2
LANES = 128
GROUP = 16
DEPTH = 12
BOTH = ("row", "col")
AHEAD = (((1,), (1,)), ((), ()))
BEHIND = (((1,), (0,)), ((), ()))
HIGH = lax.Precision.HIGHEST
F32 = jnp.float32
BF16 = jnp.bfloat16
VMEM = pl.BlockSpec(memory_space=pltpu.VMEM)
SMEM = pl.BlockSpec(memory_space=pltpu.SMEM)
PARAMS = pltpu.CompilerParams(vmem_limit_bytes=40 * 1024 * 1024)


def dot(left, right):
    return jnp.dot(left, right, precision=HIGH, preferred_element_type=F32)


def dot_t(left, right):
    return lax.dot_general(
        left, right, (((1,), (1,)), ((), ())), precision=HIGH, preferred_element_type=F32
    )


def dot_tn(left, right):
    return lax.dot_general(
        left, right, (((0,), (0,)), ((), ())), precision=HIGH, preferred_element_type=F32
    )


def lane_half():
    return lax.broadcasted_iota(jnp.int32, (NV, LANES), 1) // TILE


def narrowed(pair, mask):
    held = jnp.where(mask, pair, 0.0)
    return (held + pltpu.roll(held, TILE, 1))[:, :TILE]


def pieces(value, count):
    found = []
    for _ in range(count):
        piece = value.astype(BF16)
        value = value - piece.astype(F32)
        found.append(piece)
    return found


def product_of(picked, tile, dims, split):
    if split == 1:
        return lax.dot_general(picked.astype(BF16), tile, dims, preferred_element_type=F32)
    both = jnp.concatenate(pieces(picked, 2), axis=0)
    out = lax.dot_general(both, tile, dims, preferred_element_type=F32)
    return out[:NV] + out[NV:]


def both_halves(product, mask):
    return jnp.where(mask, jnp.concatenate([product, product], axis=1), 0.0)


def mix(coefficients, rows):
    out = coefficients[:, 0:1] * rows[0:1]
    for v in range(1, NV):
        out = out + coefficients[:, v : v + 1] * rows[v : v + 1]
    return out


def factor(gram):
    row = lax.broadcasted_iota(jnp.int32, (NV, 2 * NV), 0)
    lane = lax.broadcasted_iota(jnp.int32, (NV, 2 * NV), 1)
    unit = jnp.where(row + NV == lane, 1.0, 0.0).astype(F32)
    work = jnp.concatenate([gram, unit[:, NV:]], axis=1)
    for j in range(NV):
        scale = 1.0 / jnp.sqrt(work[j : j + 1, j : j + 1])
        scaled = work[j : j + 1, :] * scale
        column = work[:, j : j + 1] * scale
        work = jnp.where(row == j, scaled, jnp.where(row > j, work - column * scaled, work))
    return jnp.where(row <= lane, work, 0.0)[:, :NV], work[:, NV:]


def factor_of_sums(summed):
    alpha = summed[:, :NV]
    mixed = summed[:, NV : 2 * NV]
    own = summed[:, 2 * NV : 3 * NV]
    square = summed[:, 3 * NV : 4 * NV]
    gram = square - dot_tn(alpha, mixed) - dot_tn(mixed, alpha) + dot_tn(alpha, dot(own, alpha))
    return (alpha, *factor(gram))


def identity():
    row = lax.broadcasted_iota(jnp.int32, (NV, NV), 0)
    lane = lax.broadcasted_iota(jnp.int32, (NV, NV), 1)
    return jnp.where(row == lane, 1.0, 0.0).astype(F32)


def put_pairs(held, segment, pairs):
    per = held.shape[1] // LANES
    for part in range(per):
        pairs[segment * per + part] = held[:, part * LANES : (part + 1) * LANES]


def end_pairs(pairs):
    pairs[pairs.shape[0] - 1] = jnp.zeros((NV, LANES), F32)


def to_pairs(segments, pairs):
    for segment in range(segments.shape[0]):
        put_pairs(segments[segment].astype(F32), segment, pairs)
    end_pairs(pairs)


def part_rows(part):
    return pl.ds(part * 2 * NV, 2 * NV)


def put_message(message, own, sums, per):
    for segment in range(message.shape[0]):
        for part in range(per):
            mine = own[:, part * LANES : (part + 1) * LANES]
            partial = sums[segment * per + part].astype(BF16)
            message[segment, part_rows(part)] = jnp.concatenate([mine, partial], axis=0)


def segment_of(pairs, segment, per):
    parts = [pairs[segment * per + part] for part in range(per)]
    return jnp.concatenate(parts, axis=1)


def pair_scratch(count, sub):
    return pltpu.VMEM((count * sub // LANES + 1, NV, LANES), F32)


def accumulate(reads, writes, tiles, pairs, sums, dims, split=1):
    half = lane_half()
    sums[...] = jnp.zeros_like(sums)

    slots = tiles.shape[0]
    for first in range(0, slots, GROUP):
        updates = []
        for k in range(first, min(first + GROUP, slots)):
            read, write = reads[k], writes[k]
            picked = narrowed(pairs[lax.shift_right_logical(read, 1)], half == (read & 1))
            out = both_halves(product_of(picked, tiles[k], dims, split), half == (write & 1))
            updates.append((lax.shift_right_logical(write, 1), out))
        for pair, out in updates:
            sums[pair] += out


def front_kernel(rows, cols, tiles, band, block, message, band_pairs, sums):
    to_pairs(band, band_pairs)
    accumulate(cols, rows, tiles, band_pairs, sums, AHEAD)
    put_message(message, block[...].astype(BF16), sums, band.shape[2] // LANES)


def front(rows, cols, tiles, band, block, n_col):
    n_row, _, sub = band.shape
    return pl.pallas_call(
        front_kernel,
        out_shape=jax.ShapeDtypeStruct((n_col, 2 * NV * sub // LANES, LANES), BF16),
        in_specs=[SMEM, SMEM, VMEM, VMEM, VMEM],
        out_specs=VMEM,
        scratch_shapes=[pair_scratch(n_row, sub), pair_scratch(n_col, sub)],
        compiler_params=PARAMS,
        name="front_tiles",
    )(rows, cols, tiles, band, block)


def back_kernel(rows, cols, tiles, moved, back, owned, across_pairs, sums):
    per = back.shape[2] // LANES
    gathered = []
    for part in range(per):
        total = jnp.zeros((NV, LANES), F32)
        for segment in range(moved.shape[0]):
            held = moved[segment, part_rows(part)].astype(F32)
            across_pairs[segment * per + part] = held[:NV]
            total = total + held[NV:]
        gathered.append(total)
    end_pairs(across_pairs)
    owned[...] = jnp.concatenate(gathered, axis=1)
    accumulate(rows, cols, tiles, across_pairs, sums, BEHIND)
    for segment in range(back.shape[0]):
        back[segment] = segment_of(sums, segment, per)


def back(rows, cols, tiles, moved, n_row, sub):
    n_col = moved.shape[0]
    return pl.pallas_call(
        back_kernel,
        out_shape=(
            jax.ShapeDtypeStruct((n_row, NV, sub), F32),
            jax.ShapeDtypeStruct((NV, sub), F32),
        ),
        in_specs=[SMEM, SMEM, VMEM, VMEM],
        out_specs=(VMEM, VMEM),
        scratch_shapes=[pair_scratch(n_col, sub), pair_scratch(n_row, sub)],
        compiler_params=PARAMS,
        name="back_tiles",
    )(rows, cols, tiles, moved)


def rest_and_sums(owned, returned, current, prior, beta):
    image = owned[...] + jnp.sum(returned[...], axis=0)
    now = current[...]
    rest = image - dot(beta[...], prior[...])
    left = jnp.concatenate([now, rest], axis=0)
    right = jnp.concatenate([image, rest, now], axis=0)
    inner = dot_t(left, right)
    return rest, jnp.concatenate([inner[:NV], inner[NV:, NV : 2 * NV]], axis=1)


def local_kernel(owned, returned, current, prior, beta, ahead, sums):
    rest, blocks = rest_and_sums(owned, returned, current, prior, beta)
    ahead[...] = rest
    packed = [
        jnp.concatenate([blocks[v : v + 1] for v in range(part, part + 4)], axis=1)
        for part in (0, 4)
    ]
    one = jnp.concatenate(packed, axis=0)
    sums[...] = jnp.broadcast_to(one[None], sums.shape)


def local(owned, returned, current, prior, beta, copies):
    return pl.pallas_call(
        local_kernel,
        out_shape=(
            jax.ShapeDtypeStruct(current.shape, F32),
            jax.ShapeDtypeStruct((copies, 2, LANES), F32),
        ),
        in_specs=[VMEM] * 5,
        out_specs=(VMEM, VMEM),
        compiler_params=PARAMS,
        name="local_sums",
    )(owned, returned, current, prior, beta)


def carry_kernel(owned, returned, current, prior, beta, ahead, message):
    rest, blocks = rest_and_sums(owned, returned, current, prior, beta)
    ahead[...] = rest
    pad = jnp.zeros((NV, LANES - 4 * NV), F32)
    one = jnp.concatenate([rest, blocks, pad], axis=1)
    message[...] = jnp.broadcast_to(one[None], message.shape)


def carry(owned, returned, current, prior, beta, n_row):
    sub = current.shape[1]
    return pl.pallas_call(
        carry_kernel,
        out_shape=(
            jax.ShapeDtypeStruct(current.shape, F32),
            jax.ShapeDtypeStruct((n_row, NV, sub + LANES), F32),
        ),
        in_specs=[VMEM] * 5,
        out_specs=(VMEM, VMEM),
        compiler_params=PARAMS,
        name="local_carry",
    )(owned, returned, current, prior, beta)


def whiten_kernel(rows, cols, tiles, got, rest, message, band_pairs, sums):
    n_row = got.shape[0]
    sub = rest.shape[1]
    summed = jnp.sum(got[:, :, sub:], axis=0)[:, : 4 * NV]
    gram = summed[:, 3 * NV :] / float(n_row * sub)
    unit = identity()
    trace = jnp.sum(jnp.sum(gram * unit, axis=1, keepdims=True), axis=0, keepdims=True)
    upper, inverse = factor(gram + (trace * 1e-5 + 1e-30) * unit)
    lower = dot_tn(upper, unit)
    for segment in range(n_row):
        put_pairs(mix(inverse, got[segment, :, :sub]), segment, band_pairs)
    end_pairs(band_pairs)
    own = mix(inverse, rest[...]).astype(BF16)
    twice = jnp.concatenate([lower, lower], axis=1)
    beside = jnp.concatenate(pieces(summed, 3) + pieces(twice, 2), axis=1)
    accumulate(cols, rows, tiles, band_pairs, sums, AHEAD)
    per = sub // LANES
    put_message(message, own, sums, per)
    for segment in range(message.shape[0]):
        message[segment, pl.ds(2 * NV * per, NV)] = beside


def whiten(rows, cols, tiles, got, rest, n_col):
    n_row = got.shape[0]
    sub = rest.shape[1]
    return pl.pallas_call(
        whiten_kernel,
        out_shape=jax.ShapeDtypeStruct((n_col, 2 * NV * sub // LANES + NV, LANES), BF16),
        in_specs=[SMEM, SMEM, VMEM, VMEM, VMEM],
        out_specs=VMEM,
        scratch_shapes=[pair_scratch(n_row, sub), pair_scratch(n_col, sub)],
        compiler_params=PARAMS,
        name="whiten_tiles",
    )(rows, cols, tiles, got, rest)


def joined(held):
    width = 4 * NV
    return held[:, :width] + held[:, width : 2 * width] + held[:, 2 * width : 3 * width]


def settle_kernel(
    total, rows, cols, tiles, moved, before, rest, current,
    back, owned, following, upper_out, alphas, across_pairs, sums,
):
    n_col = moved.shape[0]
    sub = rest.shape[1]
    per = sub // LANES
    beside = pl.ds(2 * NV * per, NV)
    summed = jnp.zeros((NV, LANES), F32)
    for segment in range(n_col):
        summed = summed + moved[segment, beside].astype(F32)
    alpha, upper, inverse = factor_of_sums(joined(summed) / total)
    upper_out[...] = upper
    alphas[...] = jnp.zeros_like(alphas)
    alphas[0] = alpha
    turn = -dot_t(inverse, alpha)
    following[...] = dot(inverse, rest[...] - dot_tn(alpha, current[...]))
    columns = [jnp.broadcast_to(inverse[:, v : v + 1], (NV, LANES)) for v in range(NV)]
    four = 4 * NV
    lane = lax.broadcasted_iota(jnp.int32, (NV, four), 1)
    segment_lanes = (lane & NV) == 0
    turns = jnp.concatenate([turn] * 4, axis=1)

    def settle(segment, gathered):
        held = moved[segment, beside].astype(F32)
        held = held + pltpu.roll(held, 2 * NV, 1)
        change = columns[0] * held[0:1]
        for v in range(1, NV):
            change = change + columns[v] * held[v : v + 1]
        change = pltpu.roll(change, 2 * NV, 1)[:, :four]
        change = jnp.where(lane < 2 * NV, change, turns)
        high = change.astype(BF16).astype(F32)
        both = jnp.concatenate([high, change - high], axis=0)
        mask = jnp.concatenate([segment_lanes, segment_lanes], axis=0)
        left = jnp.concatenate([jnp.where(mask, both, 0.0), jnp.where(mask, 0.0, both)], axis=0)
        parts = []
        for part in range(per):
            now = moved[segment, part_rows(part)]
            past = before[segment, part_rows(part)]
            parts.append(jnp.concatenate([now, past], axis=0))
        right = jnp.concatenate(parts, axis=1)
        out = jnp.dot(left.astype(BF16), right, preferred_element_type=F32)
        put_pairs(out[:NV] + out[NV : 2 * NV], segment, across_pairs)
        return gathered + (out[2 * NV : 3 * NV] + out[3 * NV :])

    owned[...] = lax.fori_loop(0, n_col, settle, jnp.zeros((NV, sub), F32), unroll=True)
    end_pairs(across_pairs)
    accumulate(rows, cols, tiles, across_pairs, sums, BEHIND, split=2)
    for segment in range(back.shape[0]):
        back[segment] = segment_of(sums, segment, per)


def settle(rows, cols, tiles, moved, before, rest, current, total, n_row):
    n_col = moved.shape[0]
    sub = rest.shape[1]
    return pl.pallas_call(
        functools.partial(settle_kernel, total),
        out_shape=(
            jax.ShapeDtypeStruct((n_row, NV, sub), F32),
            jax.ShapeDtypeStruct((NV, sub), F32),
            jax.ShapeDtypeStruct((NV, sub), F32),
            jax.ShapeDtypeStruct((NV, NV), F32),
            jax.ShapeDtypeStruct((STEPS, NV, NV), F32),
        ),
        in_specs=[SMEM, SMEM] + [VMEM] * 5,
        out_specs=(VMEM,) * 5,
        scratch_shapes=[pair_scratch(n_col, sub), pair_scratch(n_row, sub)],
        compiler_params=PARAMS,
        name="settle_tiles",
    )(rows, cols, tiles, moved, before, rest, current)


def spread_kernel(parts, sums):
    one = jnp.sum(parts[...], axis=0)
    sums[...] = jnp.broadcast_to(one[None], sums.shape)


def spread(parts, copies):
    return pl.pallas_call(
        spread_kernel,
        out_shape=jax.ShapeDtypeStruct((copies, 2, LANES), F32),
        in_specs=[VMEM],
        out_specs=VMEM,
        compiler_params=PARAMS,
        name="spread_sums",
    )(parts)


def last_kernel(total, parts, rest, current, found, alphas, following):
    packed = jnp.sum(parts[...], axis=0) / total
    width = LANES // 4
    summed = jnp.concatenate(
        [packed[v // 4 : v // 4 + 1, v % 4 * width : (v % 4 + 1) * width] for v in range(NV)],
        axis=0,
    )
    alpha, _, inverse = factor_of_sums(summed)
    alphas[...] = found[...]
    alphas[STEPS - 1] = alpha
    following[...] = dot(inverse, rest[...] - dot_tn(alpha, current[...]))


def last(parts, rest, current, found, total):
    return pl.pallas_call(
        functools.partial(last_kernel, total),
        out_shape=(
            jax.ShapeDtypeStruct(found.shape, F32),
            jax.ShapeDtypeStruct(current.shape, F32),
        ),
        in_specs=[VMEM] * 4,
        out_specs=(VMEM, VMEM),
        compiler_params=PARAMS,
        name="last_block",
    )(parts, rest, current, found)


def swap(blocks, axis, groups=None):
    return lax.all_to_all(blocks, axis, 0, 0, tiled=True, axis_index_groups=groups)


def lines_and_rest(n_row, n_col):
    depth = DEPTH if n_col % DEPTH == 0 else n_col
    lines = [
        [(chip + core) * n_col + high + z for core in range(2) for z in range(depth)]
        for chip in range(0, n_row, 2)
        for high in range(0, n_col, depth)
    ]
    return lines, [list(rest) for rest in zip(*lines)]


def shards(tiles, tile_row, tile_col, tile_count, block, previous, coupling):
    slots = tiles.shape[0]
    sub = block.shape[1]
    n_row = lax.axis_size("row")
    n_col = lax.axis_size("col")
    total = float(sub * n_row * n_col)
    squares = tiles.reshape(slots, TILE, TILE)
    live = lax.iota(jnp.int32, slots) < tile_count[0]
    rows = jnp.where(live, tile_row, n_col * sub // TILE)
    cols = jnp.where(live, tile_col, n_row * sub // TILE)
    lines, others = lines_and_rest(n_row, n_col)

    copies = jnp.broadcast_to(block.astype(BF16)[None], (n_row, NV, sub))
    band = swap(copies, "row")
    before = swap(front(rows, cols, squares, band, block, n_col), "col")
    partial, owned = back(rows, cols, squares, before, n_row, sub)
    returned = swap(partial, "row")
    rest, message = carry(owned, returned, block, previous, coupling, n_row)

    got = swap(message, "row")
    moved = swap(whiten(rows, cols, squares, got, rest, n_col), "col")
    partial, owned, current, upper, found = settle(
        rows, cols, squares, moved, before, rest, block, total, n_row
    )
    returned = swap(partial, "row")
    rest, sums = local(owned, returned, current, block, upper, len(lines[0]))
    parts = swap(spread(swap(sums, BOTH, lines), len(others[0])), BOTH, others)
    found, current = last(parts, rest, current, found, total)
    return (current, found)


def solution(mesh):
    in_specs = (
        P(("row", "col"), None),
        P(("row", "col")),
        P(("row", "col")),
        P(("row", "col")),
        P(None, ("row", "col")),
        P(None, ("row", "col")),
        P(),
    )
    out_specs = (P(None, ("row", "col")), P())
    return jax.shard_map(shards, mesh=mesh, in_specs=in_specs, out_specs=out_specs, check_vma=False)
```

```python
import functools

import jax
import jax.numpy as jnp
from jax import lax
from jax.experimental import pallas as pl
from jax.experimental.pallas import tpu as pltpu
from jax.sharding import PartitionSpec as P

TILE = 64
NV = 8
STEPS = 2
LANES = 128
GROUP = 16
DEPTH = 12
BOTH = ("row", "col")
AHEAD = (((1,), (1,)), ((), ()))
BEHIND = (((1,), (0,)), ((), ()))
HIGH = lax.Precision.HIGHEST
F32 = jnp.float32
BF16 = jnp.bfloat16
VMEM = pl.BlockSpec(memory_space=pltpu.VMEM)
SMEM = pl.BlockSpec(memory_space=pltpu.SMEM)
PARAMS = pltpu.CompilerParams(vmem_limit_bytes=40 * 1024 * 1024)


def dot(left, right):
    return jnp.dot(left, right, precision=HIGH, preferred_element_type=F32)


def dot_t(left, right):
    return lax.dot_general(
        left, right, (((1,), (1,)), ((), ())), precision=HIGH, preferred_element_type=F32
    )


def dot_tn(left, right):
    return lax.dot_general(
        left, right, (((0,), (0,)), ((), ())), precision=HIGH, preferred_element_type=F32
    )


def lane_half():
    return lax.broadcasted_iota(jnp.int32, (NV, LANES), 1) // TILE


def narrowed(pair, mask):
    held = jnp.where(mask, pair, 0.0)
    return (held + pltpu.roll(held, TILE, 1))[:, :TILE]


def pieces(value, count):
    found = []
    for _ in range(count):
        piece = value.astype(BF16)
        value = value - piece.astype(F32)
        found.append(piece)
    return found


def product_of(picked, tile, dims, split):
    if split == 1:
        return lax.dot_general(picked.astype(BF16), tile, dims, preferred_element_type=F32)
    both = jnp.concatenate(pieces(picked, 2), axis=0)
    out = lax.dot_general(both, tile, dims, preferred_element_type=F32)
    return out[:NV] + out[NV:]


def both_halves(product, mask):
    return jnp.where(mask, jnp.concatenate([product, product], axis=1), 0.0)


def mix(coefficients, rows):
    out = coefficients[:, 0:1] * rows[0:1]
    for v in range(1, NV):
        out = out + coefficients[:, v : v + 1] * rows[v : v + 1]
    return out


def factor(gram):
    row = lax.broadcasted_iota(jnp.int32, (NV, 2 * NV), 0)
    lane = lax.broadcasted_iota(jnp.int32, (NV, 2 * NV), 1)
    unit = jnp.where(row + NV == lane, 1.0, 0.0).astype(F32)
    work = jnp.concatenate([gram, unit[:, NV:]], axis=1)
    scales = jnp.zeros((NV, 2 * NV), F32)
    for j in range(NV):
        column = work[:, j : j + 1]
        inverse = 1.0 / column[j : j + 1]
        scales = jnp.where(row == j, inverse, scales)
        work = jnp.where(row > j, work - column * (work[j : j + 1] * inverse), work)
    work = work * jnp.sqrt(scales)
    return jnp.where(row <= lane, work, 0.0)[:, :NV], work[:, NV:]


def factor_of_sums(summed):
    alpha = summed[:, :NV]
    mixed = summed[:, NV : 2 * NV]
    own = summed[:, 2 * NV : 3 * NV]
    square = summed[:, 3 * NV : 4 * NV]
    gram = square - dot_tn(alpha, mixed) - dot_tn(mixed, alpha) + dot_tn(alpha, dot(own, alpha))
    return (alpha, *factor(gram))


def identity():
    row = lax.broadcasted_iota(jnp.int32, (NV, NV), 0)
    lane = lax.broadcasted_iota(jnp.int32, (NV, NV), 1)
    return jnp.where(row == lane, 1.0, 0.0).astype(F32)


def put_pairs(held, segment, pairs):
    per = held.shape[1] // LANES
    for part in range(per):
        pairs[segment * per + part] = held[:, part * LANES : (part + 1) * LANES]


def end_pairs(pairs):
    pairs[pairs.shape[0] - 1] = jnp.zeros((NV, LANES), F32)


def to_pairs(segments, pairs):
    for segment in range(segments.shape[0]):
        put_pairs(segments[segment].astype(F32), segment, pairs)
    end_pairs(pairs)


def part_rows(part):
    return pl.ds(part * 2 * NV, 2 * NV)


def put_message(message, own, sums, per):
    for segment in range(message.shape[0]):
        for part in range(per):
            mine = own[:, part * LANES : (part + 1) * LANES]
            partial = sums[segment * per + part].astype(BF16)
            message[segment, part_rows(part)] = jnp.concatenate([mine, partial], axis=0)


def segment_of(pairs, segment, per):
    parts = [pairs[segment * per + part] for part in range(per)]
    return jnp.concatenate(parts, axis=1)


def pair_scratch(count, sub):
    return pltpu.VMEM((count * sub // LANES + 1, NV, LANES), F32)


def accumulate(reads, writes, tiles, pairs, sums, dims, split=1):
    half = lane_half()
    sums[...] = jnp.zeros_like(sums)

    slots = tiles.shape[0]
    for first in range(0, slots, GROUP):
        updates = []
        for k in range(first, min(first + GROUP, slots)):
            read, write = reads[k], writes[k]
            picked = narrowed(pairs[lax.shift_right_logical(read, 1)], half == (read & 1))
            out = both_halves(product_of(picked, tiles[k], dims, split), half == (write & 1))
            updates.append((lax.shift_right_logical(write, 1), out))
        for pair, out in updates:
            sums[pair] += out


def front_kernel(rows, cols, tiles, band, block, message, band_pairs, sums):
    to_pairs(band, band_pairs)
    accumulate(cols, rows, tiles, band_pairs, sums, AHEAD)
    put_message(message, block[...].astype(BF16), sums, band.shape[2] // LANES)


def front(rows, cols, tiles, band, block, n_col):
    n_row, _, sub = band.shape
    return pl.pallas_call(
        front_kernel,
        out_shape=jax.ShapeDtypeStruct((n_col, 2 * NV * sub // LANES, LANES), BF16),
        in_specs=[SMEM, SMEM, VMEM, VMEM, VMEM],
        out_specs=VMEM,
        scratch_shapes=[pair_scratch(n_row, sub), pair_scratch(n_col, sub)],
        compiler_params=PARAMS,
        name="front_tiles",
    )(rows, cols, tiles, band, block)


def back_kernel(rows, cols, tiles, moved, back, owned, across_pairs, sums):
    per = back.shape[2] // LANES
    gathered = []
    for part in range(per):
        total = jnp.zeros((NV, LANES), F32)
        for segment in range(moved.shape[0]):
            held = moved[segment, part_rows(part)].astype(F32)
            across_pairs[segment * per + part] = held[:NV]
            total = total + held[NV:]
        gathered.append(total)
    end_pairs(across_pairs)
    owned[...] = jnp.concatenate(gathered, axis=1)
    accumulate(rows, cols, tiles, across_pairs, sums, BEHIND)
    for segment in range(back.shape[0]):
        back[segment] = segment_of(sums, segment, per).astype(BF16)


def back(rows, cols, tiles, moved, n_row, sub):
    n_col = moved.shape[0]
    return pl.pallas_call(
        back_kernel,
        out_shape=(
            jax.ShapeDtypeStruct((n_row, NV, sub), BF16),
            jax.ShapeDtypeStruct((NV, sub), F32),
        ),
        in_specs=[SMEM, SMEM, VMEM, VMEM],
        out_specs=(VMEM, VMEM),
        scratch_shapes=[pair_scratch(n_col, sub), pair_scratch(n_row, sub)],
        compiler_params=PARAMS,
        name="back_tiles",
    )(rows, cols, tiles, moved)


def rest_and_sums(owned, returned, current, prior, beta):
    image = owned[...] + jnp.sum(returned[...].astype(F32), axis=0)
    now = current[...]
    rest = image - dot(beta[...], prior[...])
    left = jnp.concatenate([now, rest], axis=0)
    right = jnp.concatenate([image, rest, now], axis=0)
    inner = dot_t(left, right)
    return rest, jnp.concatenate([inner[:NV], inner[NV:, NV : 2 * NV]], axis=1)


def local_kernel(owned, returned, current, prior, beta, ahead, sums):
    rest, blocks = rest_and_sums(owned, returned, current, prior, beta)
    ahead[...] = rest
    packed = [
        jnp.concatenate([blocks[v : v + 1] for v in range(part, part + 4)], axis=1)
        for part in (0, 4)
    ]
    one = jnp.concatenate(packed, axis=0)
    sums[...] = jnp.broadcast_to(one[None], sums.shape)


def local(owned, returned, current, prior, beta, copies):
    return pl.pallas_call(
        local_kernel,
        out_shape=(
            jax.ShapeDtypeStruct(current.shape, F32),
            jax.ShapeDtypeStruct((copies, 2, LANES), F32),
        ),
        in_specs=[VMEM] * 5,
        out_specs=(VMEM, VMEM),
        compiler_params=PARAMS,
        name="local_sums",
    )(owned, returned, current, prior, beta)


def carry_kernel(owned, returned, current, prior, beta, ahead, message):
    rest, blocks = rest_and_sums(owned, returned, current, prior, beta)
    ahead[...] = rest
    pad = jnp.zeros((NV, LANES - 4 * NV), F32)
    one = jnp.concatenate([rest, blocks, pad], axis=1)
    message[...] = jnp.broadcast_to(one[None], message.shape)


def carry(owned, returned, current, prior, beta, n_row):
    sub = current.shape[1]
    return pl.pallas_call(
        carry_kernel,
        out_shape=(
            jax.ShapeDtypeStruct(current.shape, F32),
            jax.ShapeDtypeStruct((n_row, NV, sub + LANES), F32),
        ),
        in_specs=[VMEM] * 5,
        out_specs=(VMEM, VMEM),
        compiler_params=PARAMS,
        name="local_carry",
    )(owned, returned, current, prior, beta)


def whiten_kernel(rows, cols, tiles, got, rest, message, band_pairs, sums):
    n_row = got.shape[0]
    sub = rest.shape[1]
    summed = jnp.sum(got[:, :, sub:], axis=0)[:, : 4 * NV]
    gram = summed[:, 3 * NV :] / float(n_row * sub)
    unit = identity()
    trace = jnp.sum(jnp.sum(gram * unit, axis=1, keepdims=True), axis=0, keepdims=True)
    upper, inverse = factor(gram + (trace * 1e-5 + 1e-30) * unit)
    lower = dot_tn(upper, unit)
    for segment in range(n_row):
        put_pairs(mix(inverse, got[segment, :, :sub]), segment, band_pairs)
    end_pairs(band_pairs)
    own = mix(inverse, rest[...]).astype(BF16)
    twice = jnp.concatenate([lower, lower], axis=1)
    beside = jnp.concatenate(pieces(summed, 3) + pieces(twice, 2), axis=1)
    accumulate(cols, rows, tiles, band_pairs, sums, AHEAD, split=2)
    per = sub // LANES
    put_message(message, own, sums, per)
    for segment in range(message.shape[0]):
        message[segment, pl.ds(2 * NV * per, NV)] = beside


def whiten(rows, cols, tiles, got, rest, n_col):
    n_row = got.shape[0]
    sub = rest.shape[1]
    return pl.pallas_call(
        whiten_kernel,
        out_shape=jax.ShapeDtypeStruct((n_col, 2 * NV * sub // LANES + NV, LANES), BF16),
        in_specs=[SMEM, SMEM, VMEM, VMEM, VMEM],
        out_specs=VMEM,
        scratch_shapes=[pair_scratch(n_row, sub), pair_scratch(n_col, sub)],
        compiler_params=PARAMS,
        name="whiten_tiles",
    )(rows, cols, tiles, got, rest)


def joined(held):
    width = 4 * NV
    return held[:, :width] + held[:, width : 2 * width] + held[:, 2 * width : 3 * width]


def settle_kernel(
    total, rows, cols, tiles, moved, before, rest, current,
    back, owned, following, upper_out, alphas, across_pairs, sums,
):
    n_col = moved.shape[0]
    sub = rest.shape[1]
    per = sub // LANES
    beside = pl.ds(2 * NV * per, NV)
    summed = jnp.zeros((NV, LANES), F32)
    for segment in range(n_col):
        summed = summed + moved[segment, beside].astype(F32)
    alpha, upper, inverse = factor_of_sums(joined(summed) / total)
    upper_out[...] = upper
    alphas[...] = jnp.zeros_like(alphas)
    alphas[0] = alpha
    turn = -dot_t(inverse, alpha)
    following[...] = dot(inverse, rest[...] - dot_tn(alpha, current[...]))
    columns = [jnp.broadcast_to(inverse[:, v : v + 1], (NV, LANES)) for v in range(NV)]
    four = 4 * NV
    lane = lax.broadcasted_iota(jnp.int32, (NV, four), 1)
    segment_lanes = (lane & NV) == 0
    turns = jnp.concatenate([turn] * 4, axis=1)

    def settle(segment, gathered):
        held = moved[segment, beside].astype(F32)
        held = held + pltpu.roll(held, 2 * NV, 1)
        change = columns[0] * held[0:1]
        for v in range(1, NV):
            change = change + columns[v] * held[v : v + 1]
        change = pltpu.roll(change, 2 * NV, 1)[:, :four]
        change = jnp.where(lane < 2 * NV, change, turns)
        high = change.astype(BF16).astype(F32)
        both = jnp.concatenate([high, change - high], axis=0)
        mask = jnp.concatenate([segment_lanes, segment_lanes], axis=0)
        left = jnp.concatenate([jnp.where(mask, both, 0.0), jnp.where(mask, 0.0, both)], axis=0)
        parts = []
        for part in range(per):
            now = moved[segment, part_rows(part)]
            past = before[segment, part_rows(part)]
            parts.append(jnp.concatenate([now, past], axis=0))
        right = jnp.concatenate(parts, axis=1)
        out = jnp.dot(left.astype(BF16), right, preferred_element_type=F32)
        put_pairs(out[:NV] + out[NV : 2 * NV], segment, across_pairs)
        return gathered + (out[2 * NV : 3 * NV] + out[3 * NV :])

    owned[...] = lax.fori_loop(0, n_col, settle, jnp.zeros((NV, sub), F32), unroll=True)
    end_pairs(across_pairs)
    accumulate(rows, cols, tiles, across_pairs, sums, BEHIND, split=2)
    for segment in range(back.shape[0]):
        back[segment] = segment_of(sums, segment, per).astype(BF16)


def settle(rows, cols, tiles, moved, before, rest, current, total, n_row):
    n_col = moved.shape[0]
    sub = rest.shape[1]
    return pl.pallas_call(
        functools.partial(settle_kernel, total),
        out_shape=(
            jax.ShapeDtypeStruct((n_row, NV, sub), BF16),
            jax.ShapeDtypeStruct((NV, sub), F32),
            jax.ShapeDtypeStruct((NV, sub), F32),
            jax.ShapeDtypeStruct((NV, NV), F32),
            jax.ShapeDtypeStruct((STEPS, NV, NV), F32),
        ),
        in_specs=[SMEM, SMEM] + [VMEM] * 5,
        out_specs=(VMEM,) * 5,
        scratch_shapes=[pair_scratch(n_col, sub), pair_scratch(n_row, sub)],
        compiler_params=PARAMS,
        name="settle_tiles",
    )(rows, cols, tiles, moved, before, rest, current)


def spread_kernel(parts, sums):
    one = jnp.sum(parts[...], axis=0)
    sums[...] = jnp.broadcast_to(one[None], sums.shape)


def spread(parts, copies):
    return pl.pallas_call(
        spread_kernel,
        out_shape=jax.ShapeDtypeStruct((copies, 2, LANES), F32),
        in_specs=[VMEM],
        out_specs=VMEM,
        compiler_params=PARAMS,
        name="spread_sums",
    )(parts)


def last_kernel(total, parts, rest, current, found, alphas, following):
    packed = jnp.sum(parts[...], axis=0) / total
    width = LANES // 4
    summed = jnp.concatenate(
        [packed[v // 4 : v // 4 + 1, v % 4 * width : (v % 4 + 1) * width] for v in range(NV)],
        axis=0,
    )
    alpha, _, inverse = factor_of_sums(summed)
    alphas[...] = found[...]
    alphas[STEPS - 1] = alpha
    following[...] = dot(inverse, rest[...] - dot_tn(alpha, current[...]))


def last(parts, rest, current, found, total):
    return pl.pallas_call(
        functools.partial(last_kernel, total),
        out_shape=(
            jax.ShapeDtypeStruct(found.shape, F32),
            jax.ShapeDtypeStruct(current.shape, F32),
        ),
        in_specs=[VMEM] * 4,
        out_specs=(VMEM, VMEM),
        compiler_params=PARAMS,
        name="last_block",
    )(parts, rest, current, found)


def swap(blocks, axis, groups=None):
    return lax.all_to_all(blocks, axis, 0, 0, tiled=True, axis_index_groups=groups)


def lines_and_rest(n_row, n_col):
    depth = DEPTH if n_col % DEPTH == 0 else n_col
    lines = [
        [(chip + core) * n_col + high + z for core in range(2) for z in range(depth)]
        for chip in range(0, n_row, 2)
        for high in range(0, n_col, depth)
    ]
    return lines, [list(rest) for rest in zip(*lines)]


def shards(tiles, tile_row, tile_col, tile_count, block, previous, coupling):
    slots = tiles.shape[0]
    sub = block.shape[1]
    n_row = lax.axis_size("row")
    n_col = lax.axis_size("col")
    total = float(sub * n_row * n_col)
    squares = tiles.reshape(slots, TILE, TILE)
    live = lax.iota(jnp.int32, slots) < tile_count[0]
    rows = jnp.where(live, tile_row, n_col * sub // TILE)
    cols = jnp.where(live, tile_col, n_row * sub // TILE)
    lines, others = lines_and_rest(n_row, n_col)

    copies = jnp.broadcast_to(block.astype(BF16)[None], (n_row, NV, sub))
    band = swap(copies, "row")
    before = swap(front(rows, cols, squares, band, block, n_col), "col")
    partial, owned = back(rows, cols, squares, before, n_row, sub)
    returned = swap(partial, "row")
    rest, message = carry(owned, returned, block, previous, coupling, n_row)

    got = swap(message, "row")
    moved = swap(whiten(rows, cols, squares, got, rest, n_col), "col")
    partial, owned, current, upper, found = settle(
        rows, cols, squares, moved, before, rest, block, total, n_row
    )
    returned = swap(partial, "row")
    rest, sums = local(owned, returned, current, block, upper, len(lines[0]))
    parts = swap(spread(swap(sums, BOTH, lines), len(others[0])), BOTH, others)
    found, current = last(parts, rest, current, found, total)
    return (current, found)


def solution(mesh):
    in_specs = (
        P(("row", "col"), None),
        P(("row", "col")),
        P(("row", "col")),
        P(("row", "col")),
        P(None, ("row", "col")),
        P(None, ("row", "col")),
        P(),
    )
    out_specs = (P(None, ("row", "col")), P())
    return jax.shard_map(shards, mesh=mesh, in_specs=in_specs, out_specs=out_specs, check_vma=False)
```

```python
import functools

import jax
import jax.numpy as jnp
from jax import lax
from jax.experimental import pallas as pl
from jax.experimental.pallas import tpu as pltpu
from jax.sharding import PartitionSpec as P

TILE = 64
NV = 8
STEPS = 2
LANES = 128
GROUP = 16
DEPTH = 12
BOTH = ("row", "col")
AHEAD = (((1,), (1,)), ((), ()))
BEHIND = (((1,), (0,)), ((), ()))
HIGH = lax.Precision.HIGHEST
F32 = jnp.float32
BF16 = jnp.bfloat16
VMEM = pl.BlockSpec(memory_space=pltpu.VMEM)
SMEM = pl.BlockSpec(memory_space=pltpu.SMEM)
PARAMS = pltpu.CompilerParams(vmem_limit_bytes=40 * 1024 * 1024)


def dot(left, right):
    return jnp.dot(left, right, precision=HIGH, preferred_element_type=F32)


def dot_t(left, right):
    return lax.dot_general(
        left, right, (((1,), (1,)), ((), ())), precision=HIGH, preferred_element_type=F32
    )


def dot_tn(left, right):
    return lax.dot_general(
        left, right, (((0,), (0,)), ((), ())), precision=HIGH, preferred_element_type=F32
    )


def lane_half():
    return lax.broadcasted_iota(jnp.int32, (NV, LANES), 1) // TILE


def narrowed(pair, mask):
    held = jnp.where(mask, pair, 0.0)
    return (held + pltpu.roll(held, TILE, 1))[:, :TILE]


def pieces(value, count):
    found = []
    for _ in range(count):
        piece = value.astype(BF16)
        value = value - piece.astype(F32)
        found.append(piece)
    return found


def product_of(picked, tile, dims, split):
    if split == 1:
        return lax.dot_general(picked.astype(BF16), tile, dims, preferred_element_type=F32)
    both = jnp.concatenate(pieces(picked, 2), axis=0)
    out = lax.dot_general(both, tile, dims, preferred_element_type=F32)
    return out[:NV] + out[NV:]


def both_halves(product, mask):
    return jnp.where(mask, jnp.concatenate([product, product], axis=1), 0.0)


def mix(coefficients, rows):
    out = coefficients[:, 0:1] * rows[0:1]
    for v in range(1, NV):
        out = out + coefficients[:, v : v + 1] * rows[v : v + 1]
    return out


def factor(gram):
    row = lax.broadcasted_iota(jnp.int32, (NV, 2 * NV), 0)
    lane = lax.broadcasted_iota(jnp.int32, (NV, 2 * NV), 1)
    unit = jnp.where(row + NV == lane, 1.0, 0.0).astype(F32)
    work = jnp.concatenate([gram, unit[:, NV:]], axis=1)
    scales = jnp.zeros((NV, 2 * NV), F32)
    for j in range(NV):
        column = work[:, j : j + 1]
        inverse = 1.0 / column[j : j + 1]
        scales = jnp.where(row == j, inverse, scales)
        work = jnp.where(row > j, work - column * (work[j : j + 1] * inverse), work)
    work = work * jnp.sqrt(scales)
    return jnp.where(row <= lane, work, 0.0)[:, :NV], work[:, NV:]


def factor_of_sums(summed):
    alpha = summed[:, :NV]
    mixed = summed[:, NV : 2 * NV]
    own = summed[:, 2 * NV : 3 * NV]
    square = summed[:, 3 * NV : 4 * NV]
    gram = square - dot_tn(alpha, mixed) - dot_tn(mixed, alpha) + dot_tn(alpha, dot(own, alpha))
    return (alpha, *factor(gram))


def identity():
    row = lax.broadcasted_iota(jnp.int32, (NV, NV), 0)
    lane = lax.broadcasted_iota(jnp.int32, (NV, NV), 1)
    return jnp.where(row == lane, 1.0, 0.0).astype(F32)


def put_pairs(held, segment, pairs):
    per = held.shape[1] // LANES
    for part in range(per):
        pairs[segment * per + part] = held[:, part * LANES : (part + 1) * LANES]


def end_pairs(pairs):
    pairs[pairs.shape[0] - 1] = jnp.zeros((NV, LANES), F32)


def to_pairs(segments, pairs):
    for segment in range(segments.shape[0]):
        put_pairs(segments[segment].astype(F32), segment, pairs)
    end_pairs(pairs)


def part_rows(part):
    return pl.ds(part * 2 * NV, 2 * NV)


def put_message(message, own, sums, per):
    for segment in range(message.shape[0]):
        for part in range(per):
            mine = own[:, part * LANES : (part + 1) * LANES]
            partial = sums[segment * per + part].astype(BF16)
            message[segment, part_rows(part)] = jnp.concatenate([mine, partial], axis=0)


def segment_of(pairs, segment, per):
    parts = [pairs[segment * per + part] for part in range(per)]
    return jnp.concatenate(parts, axis=1)


def pair_scratch(count, sub):
    return pltpu.VMEM((count * sub // LANES + 1, NV, LANES), F32)


def accumulate(reads, writes, tiles, pairs, sums, dims, split=1):
    half = lane_half()
    sums[...] = jnp.zeros_like(sums)

    slots = tiles.shape[0]
    for first in range(0, slots, GROUP):
        updates = []
        for k in range(first, min(first + GROUP, slots)):
            read, write = reads[k], writes[k]
            picked = narrowed(pairs[lax.shift_right_logical(read, 1)], half == (read & 1))
            out = both_halves(product_of(picked, tiles[k], dims, split), half == (write & 1))
            updates.append((lax.shift_right_logical(write, 1), out))
        for pair, out in updates:
            sums[pair] += out


def front_kernel(rows, cols, tiles, band, block, message, band_pairs, sums):
    to_pairs(band, band_pairs)
    accumulate(cols, rows, tiles, band_pairs, sums, AHEAD)
    put_message(message, block[...].astype(BF16), sums, band.shape[2] // LANES)


def front(rows, cols, tiles, band, block, n_col):
    n_row, _, sub = band.shape
    return pl.pallas_call(
        front_kernel,
        out_shape=jax.ShapeDtypeStruct((n_col, 2 * NV * sub // LANES, LANES), BF16),
        in_specs=[SMEM, SMEM, VMEM, VMEM, VMEM],
        out_specs=VMEM,
        scratch_shapes=[pair_scratch(n_row, sub), pair_scratch(n_col, sub)],
        compiler_params=PARAMS,
        name="front_tiles",
    )(rows, cols, tiles, band, block)


def back_kernel(rows, cols, tiles, moved, back, owned, across_pairs, sums):
    per = back.shape[2] // LANES
    gathered = []
    for part in range(per):
        total = jnp.zeros((NV, LANES), F32)
        for segment in range(moved.shape[0]):
            held = moved[segment, part_rows(part)].astype(F32)
            across_pairs[segment * per + part] = held[:NV]
            total = total + held[NV:]
        gathered.append(total)
    end_pairs(across_pairs)
    owned[...] = jnp.concatenate(gathered, axis=1)
    accumulate(rows, cols, tiles, across_pairs, sums, BEHIND)
    for segment in range(back.shape[0]):
        back[segment] = segment_of(sums, segment, per).astype(BF16)


def back(rows, cols, tiles, moved, n_row, sub):
    n_col = moved.shape[0]
    return pl.pallas_call(
        back_kernel,
        out_shape=(
            jax.ShapeDtypeStruct((n_row, NV, sub), BF16),
            jax.ShapeDtypeStruct((NV, sub), F32),
        ),
        in_specs=[SMEM, SMEM, VMEM, VMEM],
        out_specs=(VMEM, VMEM),
        scratch_shapes=[pair_scratch(n_col, sub), pair_scratch(n_row, sub)],
        compiler_params=PARAMS,
        name="back_tiles",
    )(rows, cols, tiles, moved)


def rest_and_sums(owned, returned, current, prior, beta):
    image = owned[...] + jnp.sum(returned[...].astype(F32), axis=0)
    now = current[...]
    rest = image - dot(beta[...], prior[...])
    left = jnp.concatenate([now, rest], axis=0)
    right = jnp.concatenate([image, rest, now], axis=0)
    inner = dot_t(left, right)
    return rest, jnp.concatenate([inner[:NV], inner[NV:, NV : 2 * NV]], axis=1)


def local_kernel(owned, returned, current, prior, beta, ahead, sums):
    rest, blocks = rest_and_sums(owned, returned, current, prior, beta)
    ahead[...] = rest
    packed = [
        jnp.concatenate([blocks[v : v + 1] for v in range(part, part + 4)], axis=1)
        for part in (0, 4)
    ]
    one = jnp.concatenate(packed, axis=0)
    sums[...] = jnp.broadcast_to(one[None], sums.shape)


def local(owned, returned, current, prior, beta, copies):
    return pl.pallas_call(
        local_kernel,
        out_shape=(
            jax.ShapeDtypeStruct(current.shape, F32),
            jax.ShapeDtypeStruct((copies, 2, LANES), F32),
        ),
        in_specs=[VMEM] * 5,
        out_specs=(VMEM, VMEM),
        compiler_params=PARAMS,
        name="local_sums",
    )(owned, returned, current, prior, beta)


def carry_kernel(owned, returned, current, prior, beta, ahead, message):
    rest, blocks = rest_and_sums(owned, returned, current, prior, beta)
    ahead[...] = rest
    pad = jnp.zeros((NV, LANES - 4 * NV), F32)
    one = jnp.concatenate([rest, blocks, pad], axis=1)
    message[...] = jnp.broadcast_to(one[None], message.shape)


def carry(owned, returned, current, prior, beta, n_row):
    sub = current.shape[1]
    return pl.pallas_call(
        carry_kernel,
        out_shape=(
            jax.ShapeDtypeStruct(current.shape, F32),
            jax.ShapeDtypeStruct((n_row, NV, sub + LANES), F32),
        ),
        in_specs=[VMEM] * 5,
        out_specs=(VMEM, VMEM),
        compiler_params=PARAMS,
        name="local_carry",
    )(owned, returned, current, prior, beta)


def whiten_kernel(rows, cols, tiles, got, rest, message, band_pairs, sums):
    n_row = got.shape[0]
    sub = rest.shape[1]
    summed = jnp.sum(got[:, :, sub:], axis=0)[:, : 4 * NV]
    gram = summed[:, 3 * NV :] / float(n_row * sub)
    unit = identity()
    trace = jnp.sum(jnp.sum(gram * unit, axis=1, keepdims=True), axis=0, keepdims=True)
    upper, inverse = factor(gram + (trace * 1e-5 + 1e-30) * unit)
    lower = dot_tn(upper, unit)
    for segment in range(n_row):
        put_pairs(mix(inverse, got[segment, :, :sub]), segment, band_pairs)
    end_pairs(band_pairs)
    own = mix(inverse, rest[...]).astype(BF16)
    twice = jnp.concatenate([lower, lower], axis=1)
    beside = jnp.concatenate(pieces(summed, 3) + pieces(twice, 2), axis=1)
    accumulate(cols, rows, tiles, band_pairs, sums, AHEAD, split=2)
    per = sub // LANES
    put_message(message, own, sums, per)
    for segment in range(message.shape[0]):
        message[segment, pl.ds(2 * NV * per, NV)] = beside


def whiten(rows, cols, tiles, got, rest, n_col):
    n_row = got.shape[0]
    sub = rest.shape[1]
    return pl.pallas_call(
        whiten_kernel,
        out_shape=jax.ShapeDtypeStruct((n_col, 2 * NV * sub // LANES + NV, LANES), BF16),
        in_specs=[SMEM, SMEM, VMEM, VMEM, VMEM],
        out_specs=VMEM,
        scratch_shapes=[pair_scratch(n_row, sub), pair_scratch(n_col, sub)],
        compiler_params=PARAMS,
        name="whiten_tiles",
    )(rows, cols, tiles, got, rest)


def joined(held):
    width = 4 * NV
    return held[:, :width] + held[:, width : 2 * width] + held[:, 2 * width : 3 * width]


def settle_kernel(
    total, rows, cols, tiles, moved, before, rest, current,
    back, owned, following, upper_out, alphas, across_pairs, sums,
):
    n_col = moved.shape[0]
    sub = rest.shape[1]
    per = sub // LANES
    beside = pl.ds(2 * NV * per, NV)
    summed = jnp.zeros((NV, LANES), F32)
    for segment in range(n_col):
        summed = summed + moved[segment, beside].astype(F32)
    alpha, upper, inverse = factor_of_sums(joined(summed) / total)
    upper_out[...] = upper
    alphas[...] = jnp.zeros_like(alphas)
    alphas[0] = alpha
    turn = -dot_t(inverse, alpha)
    following[...] = dot(inverse, rest[...] - dot_tn(alpha, current[...]))
    columns = [jnp.broadcast_to(inverse[:, v : v + 1], (NV, LANES)) for v in range(NV)]
    four = 4 * NV
    lane = lax.broadcasted_iota(jnp.int32, (NV, four), 1)
    segment_lanes = (lane & NV) == 0
    turns = jnp.concatenate([turn] * 4, axis=1)

    def settle(segment, gathered):
        held = moved[segment, beside].astype(F32)
        held = held + pltpu.roll(held, 2 * NV, 1)
        change = columns[0] * held[0:1]
        for v in range(1, NV):
            change = change + columns[v] * held[v : v + 1]
        change = pltpu.roll(change, 2 * NV, 1)[:, :four]
        change = jnp.where(lane < 2 * NV, change, turns)
        high = change.astype(BF16).astype(F32)
        both = jnp.concatenate([high, change - high], axis=0)
        mask = jnp.concatenate([segment_lanes, segment_lanes], axis=0)
        left = jnp.concatenate([jnp.where(mask, both, 0.0), jnp.where(mask, 0.0, both)], axis=0)
        parts = []
        for part in range(per):
            now = moved[segment, part_rows(part)]
            past = before[segment, part_rows(part)]
            parts.append(jnp.concatenate([now, past], axis=0))
        right = jnp.concatenate(parts, axis=1)
        out = jnp.dot(left.astype(BF16), right, preferred_element_type=F32)
        put_pairs(out[:NV] + out[NV : 2 * NV], segment, across_pairs)
        return gathered + (out[2 * NV : 3 * NV] + out[3 * NV :])

    owned[...] = lax.fori_loop(0, n_col, settle, jnp.zeros((NV, sub), F32), unroll=True)
    end_pairs(across_pairs)
    accumulate(rows, cols, tiles, across_pairs, sums, BEHIND, split=2)
    for segment in range(back.shape[0]):
        back[segment] = segment_of(sums, segment, per).astype(BF16)


def settle(rows, cols, tiles, moved, before, rest, current, total, n_row):
    n_col = moved.shape[0]
    sub = rest.shape[1]
    return pl.pallas_call(
        functools.partial(settle_kernel, total),
        out_shape=(
            jax.ShapeDtypeStruct((n_row, NV, sub), BF16),
            jax.ShapeDtypeStruct((NV, sub), F32),
            jax.ShapeDtypeStruct((NV, sub), F32),
            jax.ShapeDtypeStruct((NV, NV), F32),
            jax.ShapeDtypeStruct((STEPS, NV, NV), F32),
        ),
        in_specs=[SMEM, SMEM] + [VMEM] * 5,
        out_specs=(VMEM,) * 5,
        scratch_shapes=[pair_scratch(n_col, sub), pair_scratch(n_row, sub)],
        compiler_params=PARAMS,
        name="settle_tiles",
    )(rows, cols, tiles, moved, before, rest, current)


def spread_kernel(parts, sums):
    one = jnp.sum(parts[...], axis=0)
    sums[...] = jnp.broadcast_to(one[None], sums.shape)


def spread(parts, copies):
    return pl.pallas_call(
        spread_kernel,
        out_shape=jax.ShapeDtypeStruct((copies, 2, LANES), F32),
        in_specs=[VMEM],
        out_specs=VMEM,
        compiler_params=PARAMS,
        name="spread_sums",
    )(parts)


def last_kernel(total, parts, rest, current, found, alphas, following):
    packed = jnp.sum(parts[...], axis=0) / total
    width = LANES // 4
    summed = jnp.concatenate(
        [packed[v // 4 : v // 4 + 1, v % 4 * width : (v % 4 + 1) * width] for v in range(NV)],
        axis=0,
    )
    alpha, _, inverse = factor_of_sums(summed)
    alphas[...] = found[...]
    alphas[STEPS - 1] = alpha
    following[...] = dot(inverse, rest[...] - dot_tn(alpha, current[...]))


def last(parts, rest, current, found, total):
    return pl.pallas_call(
        functools.partial(last_kernel, total),
        out_shape=(
            jax.ShapeDtypeStruct(found.shape, F32),
            jax.ShapeDtypeStruct(current.shape, F32),
        ),
        in_specs=[VMEM] * 4,
        out_specs=(VMEM, VMEM),
        compiler_params=PARAMS,
        name="last_block",
    )(parts, rest, current, found)


def round_kernel(block, copies, held, done):
    fetch = pltpu.make_async_copy(block, held, done)
    fetch.start()
    fetch.wait()
    copies[...] = jnp.broadcast_to(held[...].astype(BF16)[None], copies.shape)


def round_block(block, n_row):
    return pl.pallas_call(
        round_kernel,
        out_shape=jax.ShapeDtypeStruct((n_row, *block.shape), BF16),
        in_specs=[pl.BlockSpec(memory_space=pltpu.HBM)],
        out_specs=VMEM,
        scratch_shapes=[pltpu.VMEM(block.shape, F32), pltpu.SemaphoreType.DMA],
        compiler_params=pltpu.CompilerParams(vmem_limit_bytes=63 * 1024 * 1024),
        name="round_block",
    )(block)


def swap(blocks, axis, groups=None):
    return lax.all_to_all(blocks, axis, 0, 0, tiled=True, axis_index_groups=groups)


def lines_and_rest(n_row, n_col):
    depth = DEPTH if n_col % DEPTH == 0 else n_col
    lines = [
        [(chip + core) * n_col + high + z for core in range(2) for z in range(depth)]
        for chip in range(0, n_row, 2)
        for high in range(0, n_col, depth)
    ]
    return lines, [list(rest) for rest in zip(*lines)]


def shards(tiles, tile_row, tile_col, tile_count, block, previous, coupling):
    slots = tiles.shape[0]
    sub = block.shape[1]
    n_row = lax.axis_size("row")
    n_col = lax.axis_size("col")
    total = float(sub * n_row * n_col)
    squares = tiles.reshape(slots, TILE, TILE)
    live = lax.iota(jnp.int32, slots) < tile_count[0]
    rows = jnp.where(live, tile_row, n_col * sub // TILE)
    cols = jnp.where(live, tile_col, n_row * sub // TILE)
    lines, others = lines_and_rest(n_row, n_col)

    band = swap(round_block(block, n_row), "row")
    before = swap(front(rows, cols, squares, band, block, n_col), "col")
    partial, owned = back(rows, cols, squares, before, n_row, sub)
    returned = swap(partial, "row")
    rest, message = carry(owned, returned, block, previous, coupling, n_row)

    got = swap(message, "row")
    moved = swap(whiten(rows, cols, squares, got, rest, n_col), "col")
    partial, owned, current, upper, found = settle(
        rows, cols, squares, moved, before, rest, block, total, n_row
    )
    returned = swap(partial, "row")
    rest, sums = local(owned, returned, current, block, upper, len(lines[0]))
    parts = swap(spread(swap(sums, BOTH, lines), len(others[0])), BOTH, others)
    found, current = last(parts, rest, current, found, total)
    return (current, found)


def solution(mesh):
    in_specs = (
        P(("row", "col"), None),
        P(("row", "col")),
        P(("row", "col")),
        P(("row", "col")),
        P(None, ("row", "col")),
        P(None, ("row", "col")),
        P(),
    )
    out_specs = (P(None, ("row", "col")), P())
    return jax.shard_map(shards, mesh=mesh, in_specs=in_specs, out_specs=out_specs, check_vma=False)
```

```python
import functools

import jax
import jax.numpy as jnp
from jax import lax
from jax.experimental import pallas as pl
from jax.experimental.pallas import tpu as pltpu
from jax.sharding import PartitionSpec as P

TILE = 64
NV = 8
STEPS = 2
LANES = 128
GROUP = 16
DEPTH = 12
BOTH = ("row", "col")
AHEAD = (((1,), (1,)), ((), ()))
BEHIND = (((1,), (0,)), ((), ()))
HIGH = lax.Precision.HIGHEST
F32 = jnp.float32
BF16 = jnp.bfloat16
VMEM = pl.BlockSpec(memory_space=pltpu.VMEM)
SMEM = pl.BlockSpec(memory_space=pltpu.SMEM)
PARAMS = pltpu.CompilerParams(vmem_limit_bytes=40 * 1024 * 1024)


def dot(left, right):
    return jnp.dot(left, right, precision=HIGH, preferred_element_type=F32)


def dot_t(left, right):
    return lax.dot_general(
        left, right, (((1,), (1,)), ((), ())), precision=HIGH, preferred_element_type=F32
    )


def dot_tn(left, right):
    return lax.dot_general(
        left, right, (((0,), (0,)), ((), ())), precision=HIGH, preferred_element_type=F32
    )


def lane_half():
    return lax.broadcasted_iota(jnp.int32, (NV, LANES), 1) // TILE


def narrowed(pair, mask):
    held = jnp.where(mask, pair, 0.0)
    return (held + pltpu.roll(held, TILE, 1))[:, :TILE]


def pieces(value, count):
    found = []
    for _ in range(count):
        piece = value.astype(BF16)
        value = value - piece.astype(F32)
        found.append(piece)
    return found


def product_of(picked, tile, dims, split):
    if split == 1:
        return lax.dot_general(picked.astype(BF16), tile, dims, preferred_element_type=F32)
    both = jnp.concatenate(pieces(picked, 2), axis=0)
    out = lax.dot_general(both, tile, dims, preferred_element_type=F32)
    return out[:NV] + out[NV:]


def both_halves(product, mask):
    return jnp.where(mask, jnp.concatenate([product, product], axis=1), 0.0)


def mix(coefficients, rows):
    out = coefficients[:, 0:1] * rows[0:1]
    for v in range(1, NV):
        out = out + coefficients[:, v : v + 1] * rows[v : v + 1]
    return out


def factor(gram):
    row = lax.broadcasted_iota(jnp.int32, (NV, 2 * NV), 0)
    lane = lax.broadcasted_iota(jnp.int32, (NV, 2 * NV), 1)
    unit = jnp.where(row + NV == lane, 1.0, 0.0).astype(F32)
    work = jnp.concatenate([gram, unit[:, NV:]], axis=1)
    scales = jnp.zeros((NV, 2 * NV), F32)
    for j in range(NV):
        column = work[:, j : j + 1]
        inverse = 1.0 / column[j : j + 1]
        scales = jnp.where(row == j, inverse, scales)
        work = jnp.where(row > j, work - column * (work[j : j + 1] * inverse), work)
    work = work * jnp.sqrt(scales)
    return jnp.where(row <= lane, work, 0.0)[:, :NV], work[:, NV:]


def factor_of_sums(summed):
    alpha = summed[:, :NV]
    mixed = summed[:, NV : 2 * NV]
    own = summed[:, 2 * NV : 3 * NV]
    square = summed[:, 3 * NV : 4 * NV]
    gram = square + dot_tn(alpha, mix(own, alpha) - mixed) - dot_tn(mixed, alpha)
    return (alpha, *factor(gram))


def identity():
    row = lax.broadcasted_iota(jnp.int32, (NV, NV), 0)
    lane = lax.broadcasted_iota(jnp.int32, (NV, NV), 1)
    return jnp.where(row == lane, 1.0, 0.0).astype(F32)


def put_pairs(held, segment, pairs):
    per = held.shape[1] // LANES
    for part in range(per):
        pairs[segment * per + part] = held[:, part * LANES : (part + 1) * LANES]


def end_pairs(pairs):
    pairs[pairs.shape[0] - 1] = jnp.zeros((NV, LANES), F32)


def to_pairs(segments, pairs):
    for segment in range(segments.shape[0]):
        put_pairs(segments[segment].astype(F32), segment, pairs)
    end_pairs(pairs)


def part_rows(part):
    return pl.ds(part * 2 * NV, 2 * NV)


def put_message(message, own, sums, per):
    for segment in range(message.shape[0]):
        for part in range(per):
            mine = own[:, part * LANES : (part + 1) * LANES]
            partial = sums[segment * per + part].astype(BF16)
            message[segment, part_rows(part)] = jnp.concatenate([mine, partial], axis=0)


def segment_of(pairs, segment, per):
    parts = [pairs[segment * per + part] for part in range(per)]
    return jnp.concatenate(parts, axis=1)


def pair_scratch(count, sub):
    return pltpu.VMEM((count * sub // LANES + 1, NV, LANES), F32)


def accumulate(reads, writes, tiles, pairs, sums, dims, split=1):
    half = lane_half()
    sums[...] = jnp.zeros_like(sums)

    slots = tiles.shape[0]
    for first in range(0, slots, GROUP):
        updates = []
        for k in range(first, min(first + GROUP, slots)):
            read, write = reads[k], writes[k]
            picked = narrowed(pairs[lax.shift_right_logical(read, 1)], half == (read & 1))
            out = both_halves(product_of(picked, tiles[k], dims, split), half == (write & 1))
            updates.append((lax.shift_right_logical(write, 1), out))
        for pair, out in updates:
            sums[pair] += out


def front_kernel(rows, cols, tiles, band, block, message, band_pairs, sums):
    to_pairs(band, band_pairs)
    accumulate(cols, rows, tiles, band_pairs, sums, AHEAD)
    put_message(message, block[...].astype(BF16), sums, band.shape[2] // LANES)


def front(rows, cols, tiles, band, block, n_col):
    n_row, _, sub = band.shape
    return pl.pallas_call(
        front_kernel,
        out_shape=jax.ShapeDtypeStruct((n_col, 2 * NV * sub // LANES, LANES), BF16),
        in_specs=[SMEM, SMEM, VMEM, VMEM, VMEM],
        out_specs=VMEM,
        scratch_shapes=[pair_scratch(n_row, sub), pair_scratch(n_col, sub)],
        compiler_params=PARAMS,
        name="front_tiles",
    )(rows, cols, tiles, band, block)


def back_kernel(rows, cols, tiles, moved, back, owned, across_pairs, sums):
    per = back.shape[2] // LANES
    gathered = []
    for part in range(per):
        total = jnp.zeros((NV, LANES), F32)
        for segment in range(moved.shape[0]):
            held = moved[segment, part_rows(part)].astype(F32)
            across_pairs[segment * per + part] = held[:NV]
            total = total + held[NV:]
        gathered.append(total)
    end_pairs(across_pairs)
    owned[...] = jnp.concatenate(gathered, axis=1)
    accumulate(rows, cols, tiles, across_pairs, sums, BEHIND)
    for segment in range(back.shape[0]):
        back[segment] = segment_of(sums, segment, per).astype(BF16)


def back(rows, cols, tiles, moved, n_row, sub):
    n_col = moved.shape[0]
    return pl.pallas_call(
        back_kernel,
        out_shape=(
            jax.ShapeDtypeStruct((n_row, NV, sub), BF16),
            jax.ShapeDtypeStruct((NV, sub), F32),
        ),
        in_specs=[SMEM, SMEM, VMEM, VMEM],
        out_specs=(VMEM, VMEM),
        scratch_shapes=[pair_scratch(n_col, sub), pair_scratch(n_row, sub)],
        compiler_params=PARAMS,
        name="back_tiles",
    )(rows, cols, tiles, moved)


def rest_and_sums(owned, returned, current, prior, beta):
    image = owned[...] + jnp.sum(returned[...].astype(F32), axis=0)
    now = current[...]
    rest = image - dot(beta[...], prior[...])
    left = jnp.concatenate([now, rest], axis=0)
    right = jnp.concatenate([image, rest, now], axis=0)
    inner = dot_t(left, right)
    return rest, jnp.concatenate([inner[:NV], inner[NV:, NV : 2 * NV]], axis=1)


def local_kernel(owned, returned, current, prior, beta, ahead, sums):
    rest, blocks = rest_and_sums(owned, returned, current, prior, beta)
    ahead[...] = rest
    packed = [
        jnp.concatenate([blocks[v : v + 1] for v in range(part, part + 4)], axis=1)
        for part in (0, 4)
    ]
    one = jnp.concatenate(packed, axis=0)
    sums[...] = jnp.broadcast_to(one[None], sums.shape)


def local(owned, returned, current, prior, beta, copies):
    return pl.pallas_call(
        local_kernel,
        out_shape=(
            jax.ShapeDtypeStruct(current.shape, F32),
            jax.ShapeDtypeStruct((copies, 2, LANES), F32),
        ),
        in_specs=[VMEM] * 5,
        out_specs=(VMEM, VMEM),
        compiler_params=PARAMS,
        name="local_sums",
    )(owned, returned, current, prior, beta)


def carry_kernel(owned, returned, current, prior, beta, ahead, message):
    rest, blocks = rest_and_sums(owned, returned, current, prior, beta)
    ahead[...] = rest
    pad = jnp.zeros((NV, LANES - 4 * NV), F32)
    one = jnp.concatenate([rest, blocks, pad], axis=1)
    message[...] = jnp.broadcast_to(one[None], message.shape)


def carry(owned, returned, current, prior, beta, n_row):
    sub = current.shape[1]
    return pl.pallas_call(
        carry_kernel,
        out_shape=(
            jax.ShapeDtypeStruct(current.shape, F32),
            jax.ShapeDtypeStruct((n_row, NV, sub + LANES), F32),
        ),
        in_specs=[VMEM] * 5,
        out_specs=(VMEM, VMEM),
        compiler_params=PARAMS,
        name="local_carry",
    )(owned, returned, current, prior, beta)


def whiten_kernel(rows, cols, tiles, got, rest, message, band_pairs, sums):
    n_row = got.shape[0]
    sub = rest.shape[1]
    summed = jnp.sum(got[:, :, sub:], axis=0)[:, : 4 * NV]
    gram = summed[:, 3 * NV :] / float(n_row * sub)
    unit = identity()
    trace = jnp.sum(jnp.sum(gram * unit, axis=1, keepdims=True), axis=0, keepdims=True)
    upper, inverse = factor(gram + (trace * 1e-5 + 1e-30) * unit)
    lower = dot_tn(upper, unit)
    for segment in range(n_row):
        put_pairs(mix(inverse, got[segment, :, :sub]), segment, band_pairs)
    end_pairs(band_pairs)
    own = mix(inverse, rest[...]).astype(BF16)
    twice = jnp.concatenate([lower, lower], axis=1)
    beside = jnp.concatenate(pieces(summed, 3) + pieces(twice, 2), axis=1)
    accumulate(cols, rows, tiles, band_pairs, sums, AHEAD, split=2)
    per = sub // LANES
    put_message(message, own, sums, per)
    for segment in range(message.shape[0]):
        message[segment, pl.ds(2 * NV * per, NV)] = beside


def whiten(rows, cols, tiles, got, rest, n_col):
    n_row = got.shape[0]
    sub = rest.shape[1]
    return pl.pallas_call(
        whiten_kernel,
        out_shape=jax.ShapeDtypeStruct((n_col, 2 * NV * sub // LANES + NV, LANES), BF16),
        in_specs=[SMEM, SMEM, VMEM, VMEM, VMEM],
        out_specs=VMEM,
        scratch_shapes=[pair_scratch(n_row, sub), pair_scratch(n_col, sub)],
        compiler_params=PARAMS,
        name="whiten_tiles",
    )(rows, cols, tiles, got, rest)


def joined(held):
    width = 4 * NV
    return held[:, :width] + held[:, width : 2 * width] + held[:, 2 * width : 3 * width]


def settle_kernel(
    total, rows, cols, tiles, moved, before, rest, current,
    back, owned, following, upper_out, alphas, across_pairs, sums,
):
    n_col = moved.shape[0]
    sub = rest.shape[1]
    per = sub // LANES
    beside = pl.ds(2 * NV * per, NV)
    summed = jnp.zeros((NV, LANES), F32)
    for segment in range(n_col):
        summed = summed + moved[segment, beside].astype(F32)
    alpha, upper, inverse = factor_of_sums(joined(summed) / total)
    upper_out[...] = upper
    alphas[...] = jnp.zeros_like(alphas)
    alphas[0] = alpha
    turn = -dot_t(inverse, alpha)
    following[...] = mix(inverse, rest[...] - dot_tn(alpha, current[...]))
    columns = [jnp.broadcast_to(inverse[:, v : v + 1], (NV, LANES)) for v in range(NV)]
    four = 4 * NV
    lane = lax.broadcasted_iota(jnp.int32, (NV, four), 1)
    segment_lanes = (lane & NV) == 0
    turns = jnp.concatenate([turn] * 4, axis=1)

    def settle(segment, gathered):
        held = moved[segment, beside].astype(F32)
        held = held + pltpu.roll(held, 2 * NV, 1)
        change = columns[0] * held[0:1]
        for v in range(1, NV):
            change = change + columns[v] * held[v : v + 1]
        change = pltpu.roll(change, 2 * NV, 1)[:, :four]
        change = jnp.where(lane < 2 * NV, change, turns)
        high = change.astype(BF16).astype(F32)
        both = jnp.concatenate([high, change - high], axis=0)
        mask = jnp.concatenate([segment_lanes, segment_lanes], axis=0)
        left = jnp.concatenate([jnp.where(mask, both, 0.0), jnp.where(mask, 0.0, both)], axis=0)
        parts = []
        for part in range(per):
            now = moved[segment, part_rows(part)]
            past = before[segment, part_rows(part)]
            parts.append(jnp.concatenate([now, past], axis=0))
        right = jnp.concatenate(parts, axis=1)
        out = jnp.dot(left.astype(BF16), right, preferred_element_type=F32)
        put_pairs(out[:NV] + out[NV : 2 * NV], segment, across_pairs)
        return gathered + (out[2 * NV : 3 * NV] + out[3 * NV :])

    owned[...] = lax.fori_loop(0, n_col, settle, jnp.zeros((NV, sub), F32), unroll=True)
    end_pairs(across_pairs)
    accumulate(rows, cols, tiles, across_pairs, sums, BEHIND, split=2)
    for segment in range(back.shape[0]):
        back[segment] = segment_of(sums, segment, per).astype(BF16)


def settle(rows, cols, tiles, moved, before, rest, current, total, n_row):
    n_col = moved.shape[0]
    sub = rest.shape[1]
    return pl.pallas_call(
        functools.partial(settle_kernel, total),
        out_shape=(
            jax.ShapeDtypeStruct((n_row, NV, sub), BF16),
            jax.ShapeDtypeStruct((NV, sub), F32),
            jax.ShapeDtypeStruct((NV, sub), F32),
            jax.ShapeDtypeStruct((NV, NV), F32),
            jax.ShapeDtypeStruct((STEPS, NV, NV), F32),
        ),
        in_specs=[SMEM, SMEM] + [VMEM] * 5,
        out_specs=(VMEM,) * 5,
        scratch_shapes=[pair_scratch(n_col, sub), pair_scratch(n_row, sub)],
        compiler_params=PARAMS,
        name="settle_tiles",
    )(rows, cols, tiles, moved, before, rest, current)


def spread_kernel(parts, sums):
    one = jnp.sum(parts[...], axis=0)
    sums[...] = jnp.broadcast_to(one[None], sums.shape)


def spread(parts, copies):
    return pl.pallas_call(
        spread_kernel,
        out_shape=jax.ShapeDtypeStruct((copies, 2, LANES), F32),
        in_specs=[VMEM],
        out_specs=VMEM,
        compiler_params=PARAMS,
        name="spread_sums",
    )(parts)


def last_kernel(total, parts, rest, current, found, alphas, following):
    packed = jnp.sum(parts[...], axis=0) / total
    width = LANES // 4
    summed = jnp.concatenate(
        [packed[v // 4 : v // 4 + 1, v % 4 * width : (v % 4 + 1) * width] for v in range(NV)],
        axis=0,
    )
    alpha, _, inverse = factor_of_sums(summed)
    alphas[...] = found[...]
    alphas[STEPS - 1] = alpha
    following[...] = mix(inverse, rest[...] - dot_tn(alpha, current[...]))


def last(parts, rest, current, found, total):
    return pl.pallas_call(
        functools.partial(last_kernel, total),
        out_shape=(
            jax.ShapeDtypeStruct(found.shape, F32),
            jax.ShapeDtypeStruct(current.shape, F32),
        ),
        in_specs=[VMEM] * 4,
        out_specs=(VMEM, VMEM),
        compiler_params=PARAMS,
        name="last_block",
    )(parts, rest, current, found)


def swap(blocks, axis, groups=None):
    return lax.all_to_all(blocks, axis, 0, 0, tiled=True, axis_index_groups=groups)


def lines_and_rest(n_row, n_col):
    depth = DEPTH if n_col % DEPTH == 0 else n_col
    lines = [
        [(chip + core) * n_col + high + z for core in range(2) for z in range(depth)]
        for chip in range(0, n_row, 2)
        for high in range(0, n_col, depth)
    ]
    return lines, [list(rest) for rest in zip(*lines)]


def shards(tiles, tile_row, tile_col, tile_count, block, previous, coupling):
    slots = tiles.shape[0]
    sub = block.shape[1]
    n_row = lax.axis_size("row")
    n_col = lax.axis_size("col")
    total = float(sub * n_row * n_col)
    squares = tiles.reshape(slots, TILE, TILE)
    live = lax.iota(jnp.int32, slots) < tile_count[0]
    rows = jnp.where(live, tile_row, n_col * sub // TILE)
    cols = jnp.where(live, tile_col, n_row * sub // TILE)
    lines, others = lines_and_rest(n_row, n_col)

    copies = jnp.broadcast_to(block.astype(BF16)[None], (n_row, NV, sub))
    band = swap(copies, "row")
    before = swap(front(rows, cols, squares, band, block, n_col), "col")
    partial, owned = back(rows, cols, squares, before, n_row, sub)
    returned = swap(partial, "row")
    rest, message = carry(owned, returned, block, previous, coupling, n_row)

    got = swap(message, "row")
    moved = swap(whiten(rows, cols, squares, got, rest, n_col), "col")
    partial, owned, current, upper, found = settle(
        rows, cols, squares, moved, before, rest, block, total, n_row
    )
    returned = swap(partial, "row")
    rest, sums = local(owned, returned, current, block, upper, len(lines[0]))
    parts = swap(spread(swap(sums, BOTH, lines), len(others[0])), BOTH, others)
    found, current = last(parts, rest, current, found, total)
    return (current, found)


def solution(mesh):
    in_specs = (
        P(("row", "col"), None),
        P(("row", "col")),
        P(("row", "col")),
        P(("row", "col")),
        P(None, ("row", "col")),
        P(None, ("row", "col")),
        P(),
    )
    out_specs = (P(None, ("row", "col")), P())
    return jax.shard_map(shards, mesh=mesh, in_specs=in_specs, out_specs=out_specs, check_vma=False)
```

```python
import functools

import jax
import jax.numpy as jnp
from jax import lax
from jax.experimental import pallas as pl
from jax.experimental.pallas import tpu as pltpu
from jax.sharding import PartitionSpec as P

TILE = 64
NV = 8
STEPS = 2
LANES = 128
GROUP = 16
DEPTH = 12
BOTH = ("row", "col")
AHEAD = (((1,), (1,)), ((), ()))
BEHIND = (((1,), (0,)), ((), ()))
HIGH = lax.Precision.HIGHEST
F32 = jnp.float32
BF16 = jnp.bfloat16
VMEM = pl.BlockSpec(memory_space=pltpu.VMEM)
SMEM = pl.BlockSpec(memory_space=pltpu.SMEM)
PARAMS = pltpu.CompilerParams(vmem_limit_bytes=40 * 1024 * 1024)


def dot(left, right):
    return jnp.dot(left, right, precision=HIGH, preferred_element_type=F32)


def dot_t(left, right):
    return lax.dot_general(
        left, right, (((1,), (1,)), ((), ())), precision=HIGH, preferred_element_type=F32
    )


def dot_tn(left, right):
    return lax.dot_general(
        left, right, (((0,), (0,)), ((), ())), precision=HIGH, preferred_element_type=F32
    )


def lane_half():
    return lax.broadcasted_iota(jnp.int32, (NV, LANES), 1) // TILE


def narrowed(pair, mask):
    held = jnp.where(mask, pair, 0.0)
    return (held + pltpu.roll(held, TILE, 1))[:, :TILE]


def pieces(value, count):
    found = []
    for _ in range(count):
        piece = value.astype(BF16)
        value = value - piece.astype(F32)
        found.append(piece)
    return found


def product_of(picked, tile, dims, split):
    if split == 1:
        return lax.dot_general(picked.astype(BF16), tile, dims, preferred_element_type=F32)
    both = jnp.concatenate(pieces(picked, 2), axis=0)
    out = lax.dot_general(both, tile, dims, preferred_element_type=F32)
    return out[:NV] + out[NV:]


def both_halves(product, mask):
    return jnp.where(mask, jnp.concatenate([product, product], axis=1), 0.0)


def mix(coefficients, rows):
    out = coefficients[:, 0:1] * rows[0:1]
    for v in range(1, NV):
        out = out + coefficients[:, v : v + 1] * rows[v : v + 1]
    return out


def factor(gram):
    row = lax.broadcasted_iota(jnp.int32, (NV, 2 * NV), 0)
    lane = lax.broadcasted_iota(jnp.int32, (NV, 2 * NV), 1)
    unit = jnp.where(row + NV == lane, 1.0, 0.0).astype(F32)
    work = jnp.concatenate([gram, unit[:, NV:]], axis=1)
    scales = jnp.zeros((NV, 2 * NV), F32)
    for j in range(NV):
        column = work[:, j : j + 1]
        inverse = 1.0 / column[j : j + 1]
        scales = jnp.where(row == j, inverse, scales)
        work = jnp.where(row > j, work - column * (work[j : j + 1] * inverse), work)
    work = work * jnp.sqrt(scales)
    return jnp.where(row <= lane, work, 0.0)[:, :NV], work[:, NV:]


def factor_of_sums(summed):
    alpha = summed[:, :NV]
    mixed = summed[:, NV : 2 * NV]
    own = summed[:, 2 * NV : 3 * NV]
    square = summed[:, 3 * NV : 4 * NV]
    gram = square + dot_tn(alpha, mix(own, alpha) - mixed) - dot_tn(mixed, alpha)
    return (alpha, *factor(gram))


def identity():
    row = lax.broadcasted_iota(jnp.int32, (NV, NV), 0)
    lane = lax.broadcasted_iota(jnp.int32, (NV, NV), 1)
    return jnp.where(row == lane, 1.0, 0.0).astype(F32)


def put_pairs(held, segment, pairs):
    per = held.shape[1] // LANES
    for part in range(per):
        pairs[segment * per + part] = held[:, part * LANES : (part + 1) * LANES]


def end_pairs(pairs):
    pairs[pairs.shape[0] - 1] = jnp.zeros((NV, LANES), F32)


def to_pairs(segments, pairs):
    for segment in range(segments.shape[0]):
        put_pairs(segments[segment].astype(F32), segment, pairs)
    end_pairs(pairs)


def part_rows(part):
    return pl.ds(part * 2 * NV, 2 * NV)


def put_message(message, own, sums, per):
    for segment in range(message.shape[0]):
        for part in range(per):
            mine = own[:, part * LANES : (part + 1) * LANES]
            partial = sums[segment * per + part].astype(BF16)
            message[segment, part_rows(part)] = jnp.concatenate([mine, partial], axis=0)


def segment_of(pairs, segment, per):
    parts = [pairs[segment * per + part] for part in range(per)]
    return jnp.concatenate(parts, axis=1)


def pair_scratch(count, sub):
    return pltpu.VMEM((count * sub // LANES + 1, NV, LANES), F32)


def accumulate(reads, writes, tiles, pairs, sums, dims, split=1):
    half = lane_half()
    sums[...] = jnp.zeros_like(sums)

    slots = tiles.shape[0]
    for first in range(0, slots, GROUP):
        updates = []
        for k in range(first, min(first + GROUP, slots)):
            read, write = reads[k], writes[k]
            picked = narrowed(pairs[lax.shift_right_logical(read, 1)], half == (read & 1))
            out = both_halves(product_of(picked, tiles[k], dims, split), half == (write & 1))
            updates.append((lax.shift_right_logical(write, 1), out))
        for pair, out in updates:
            sums[pair] += out


def front_kernel(rows, cols, tiles, band, block, message, band_pairs, sums):
    to_pairs(band, band_pairs)
    accumulate(cols, rows, tiles, band_pairs, sums, AHEAD)
    put_message(message, block[...].astype(BF16), sums, band.shape[2] // LANES)


def front(rows, cols, tiles, band, block, n_col):
    n_row, _, sub = band.shape
    return pl.pallas_call(
        front_kernel,
        out_shape=jax.ShapeDtypeStruct((n_col, 2 * NV * sub // LANES, LANES), BF16),
        in_specs=[SMEM, SMEM, VMEM, VMEM, VMEM],
        out_specs=VMEM,
        scratch_shapes=[pair_scratch(n_row, sub), pair_scratch(n_col, sub)],
        compiler_params=PARAMS,
        name="front_tiles",
    )(rows, cols, tiles, band, block)


def back_kernel(rows, cols, tiles, moved, back, owned, across_pairs, sums):
    per = back.shape[2] // LANES
    gathered = []
    for part in range(per):
        total = jnp.zeros((NV, LANES), F32)
        for segment in range(moved.shape[0]):
            held = moved[segment, part_rows(part)].astype(F32)
            across_pairs[segment * per + part] = held[:NV]
            total = total + held[NV:]
        gathered.append(total)
    end_pairs(across_pairs)
    owned[...] = jnp.concatenate(gathered, axis=1)
    accumulate(rows, cols, tiles, across_pairs, sums, BEHIND)
    for segment in range(back.shape[0]):
        back[segment] = segment_of(sums, segment, per).astype(BF16)


def back(rows, cols, tiles, moved, n_row, sub):
    n_col = moved.shape[0]
    return pl.pallas_call(
        back_kernel,
        out_shape=(
            jax.ShapeDtypeStruct((n_row, NV, sub), BF16),
            jax.ShapeDtypeStruct((NV, sub), F32),
        ),
        in_specs=[SMEM, SMEM, VMEM, VMEM],
        out_specs=(VMEM, VMEM),
        scratch_shapes=[pair_scratch(n_col, sub), pair_scratch(n_row, sub)],
        compiler_params=PARAMS,
        name="back_tiles",
    )(rows, cols, tiles, moved)


def rest_and_sums(owned, returned, current, prior, beta):
    image = owned[...] + jnp.sum(returned[...].astype(F32), axis=0)
    now = current[...]
    rest = image - dot(beta[...], prior[...])
    left = jnp.concatenate([now, rest], axis=0)
    right = jnp.concatenate([image, rest, now], axis=0)
    inner = dot_t(left, right)
    return rest, jnp.concatenate([inner[:NV], inner[NV:, NV : 2 * NV]], axis=1)


def local_kernel(owned, returned, current, prior, beta, ahead, sums):
    rest, blocks = rest_and_sums(owned, returned, current, prior, beta)
    ahead[...] = rest
    packed = [
        jnp.concatenate([blocks[v : v + 1] for v in range(part, part + 4)], axis=1)
        for part in (0, 4)
    ]
    one = jnp.concatenate(packed, axis=0)
    sums[...] = jnp.broadcast_to(one[None], sums.shape)


def local(owned, returned, current, prior, beta, copies):
    return pl.pallas_call(
        local_kernel,
        out_shape=(
            jax.ShapeDtypeStruct(current.shape, F32),
            jax.ShapeDtypeStruct((copies, 2, LANES), F32),
        ),
        in_specs=[VMEM] * 5,
        out_specs=(VMEM, VMEM),
        compiler_params=PARAMS,
        name="local_sums",
    )(owned, returned, current, prior, beta)


def carry_kernel(owned, returned, current, prior, beta, ahead, message):
    rest, blocks = rest_and_sums(owned, returned, current, prior, beta)
    ahead[...] = rest
    pad = jnp.zeros((NV, LANES - 4 * NV), F32)
    one = jnp.concatenate([rest, blocks, pad], axis=1)
    message[...] = jnp.broadcast_to(one[None], message.shape)


def carry(owned, returned, current, prior, beta, n_row):
    sub = current.shape[1]
    return pl.pallas_call(
        carry_kernel,
        out_shape=(
            jax.ShapeDtypeStruct(current.shape, F32),
            jax.ShapeDtypeStruct((n_row, NV, sub + LANES), F32),
        ),
        in_specs=[VMEM] * 5,
        out_specs=(VMEM, VMEM),
        compiler_params=PARAMS,
        name="local_carry",
    )(owned, returned, current, prior, beta)


def whiten_kernel(rows, cols, tiles, got, rest, message, band_pairs, sums):
    n_row = got.shape[0]
    sub = rest.shape[1]
    summed = jnp.sum(got[:, :, sub:], axis=0)[:, : 4 * NV]
    gram = summed[:, 3 * NV :] / float(n_row * sub)
    unit = identity()
    trace = jnp.sum(jnp.sum(gram * unit, axis=1, keepdims=True), axis=0, keepdims=True)
    upper, inverse = factor(gram + (trace * 1e-5 + 1e-30) * unit)
    lower = dot_tn(upper, unit)
    for segment in range(n_row):
        put_pairs(mix(inverse, got[segment, :, :sub]), segment, band_pairs)
    end_pairs(band_pairs)
    own = mix(inverse, rest[...]).astype(BF16)
    twice = jnp.concatenate([lower, lower], axis=1)
    beside = jnp.concatenate(pieces(summed, 3) + pieces(twice, 2), axis=1)
    accumulate(cols, rows, tiles, band_pairs, sums, AHEAD, split=2)
    per = sub // LANES
    put_message(message, own, sums, per)
    for segment in range(message.shape[0]):
        message[segment, pl.ds(2 * NV * per, NV)] = beside


def whiten(rows, cols, tiles, got, rest, n_col):
    n_row = got.shape[0]
    sub = rest.shape[1]
    return pl.pallas_call(
        whiten_kernel,
        out_shape=jax.ShapeDtypeStruct((n_col, 2 * NV * sub // LANES + NV, LANES), BF16),
        in_specs=[SMEM, SMEM, VMEM, VMEM, VMEM],
        out_specs=VMEM,
        scratch_shapes=[pair_scratch(n_row, sub), pair_scratch(n_col, sub)],
        compiler_params=PARAMS,
        name="whiten_tiles",
    )(rows, cols, tiles, got, rest)


def joined(held):
    width = 4 * NV
    return held[:, :width] + held[:, width : 2 * width] + held[:, 2 * width : 3 * width]


def settle_kernel(
    total, rows, cols, tiles, moved, before, rest, current,
    back, owned, following, upper_out, alphas, across_pairs, sums,
):
    n_col = moved.shape[0]
    sub = rest.shape[1]
    per = sub // LANES
    beside = pl.ds(2 * NV * per, NV)
    summed = jnp.zeros((NV, LANES), F32)
    for segment in range(n_col):
        summed = summed + moved[segment, beside].astype(F32)
    alpha, upper, inverse = factor_of_sums(joined(summed) / total)
    upper_out[...] = upper
    alphas[...] = jnp.zeros_like(alphas)
    alphas[0] = alpha
    turn = -dot_t(inverse, alpha)
    following[...] = mix(inverse, rest[...] - dot_tn(alpha, current[...]))
    columns = [jnp.broadcast_to(inverse[:, v : v + 1], (NV, LANES)) for v in range(NV)]
    four = 4 * NV
    lane = lax.broadcasted_iota(jnp.int32, (NV, four), 1)
    segment_lanes = (lane & NV) == 0
    turns = jnp.concatenate([turn] * 4, axis=1)

    def settle(segment, gathered):
        held = moved[segment, beside].astype(F32)
        held = held + pltpu.roll(held, 2 * NV, 1)
        change = columns[0] * held[0:1]
        for v in range(1, NV):
            change = change + columns[v] * held[v : v + 1]
        change = pltpu.roll(change, 2 * NV, 1)[:, :four]
        change = jnp.where(lane < 2 * NV, change, turns)
        high = change.astype(BF16).astype(F32)
        both = jnp.concatenate([high, change - high], axis=0)
        mask = jnp.concatenate([segment_lanes, segment_lanes], axis=0)
        left = jnp.concatenate([jnp.where(mask, both, 0.0), jnp.where(mask, 0.0, both)], axis=0)
        parts = []
        for part in range(per):
            now = moved[segment, part_rows(part)]
            past = before[segment, part_rows(part)]
            parts.append(jnp.concatenate([now, past], axis=0))
        right = jnp.concatenate(parts, axis=1)
        out = jnp.dot(left.astype(BF16), right, preferred_element_type=F32)
        put_pairs(out[:NV] + out[NV : 2 * NV], segment, across_pairs)
        return gathered + (out[2 * NV : 3 * NV] + out[3 * NV :])

    owned[...] = lax.fori_loop(0, n_col, settle, jnp.zeros((NV, sub), F32), unroll=True)
    end_pairs(across_pairs)
    accumulate(rows, cols, tiles, across_pairs, sums, BEHIND, split=2)
    for segment in range(back.shape[0]):
        back[segment] = segment_of(sums, segment, per).astype(BF16)


def settle(rows, cols, tiles, moved, before, rest, current, total, n_row):
    n_col = moved.shape[0]
    sub = rest.shape[1]
    return pl.pallas_call(
        functools.partial(settle_kernel, total),
        out_shape=(
            jax.ShapeDtypeStruct((n_row, NV, sub), BF16),
            jax.ShapeDtypeStruct((NV, sub), F32),
            jax.ShapeDtypeStruct((NV, sub), F32),
            jax.ShapeDtypeStruct((NV, NV), F32),
            jax.ShapeDtypeStruct((STEPS, NV, NV), F32),
        ),
        in_specs=[SMEM, SMEM] + [VMEM] * 5,
        out_specs=(VMEM,) * 5,
        scratch_shapes=[pair_scratch(n_col, sub), pair_scratch(n_row, sub)],
        compiler_params=PARAMS,
        name="settle_tiles",
    )(rows, cols, tiles, moved, before, rest, current)


def spread_kernel(parts, sums):
    one = jnp.sum(parts[...], axis=0)
    sums[...] = jnp.broadcast_to(one[None], sums.shape)


def spread(parts, copies):
    return pl.pallas_call(
        spread_kernel,
        out_shape=jax.ShapeDtypeStruct((copies, 2, LANES), F32),
        in_specs=[VMEM],
        out_specs=VMEM,
        compiler_params=PARAMS,
        name="spread_sums",
    )(parts)


def last_kernel(total, parts, rest, current, found, alphas, following):
    packed = jnp.sum(parts[...], axis=0) / total
    width = LANES // 4
    summed = jnp.concatenate(
        [packed[v // 4 : v // 4 + 1, v % 4 * width : (v % 4 + 1) * width] for v in range(NV)],
        axis=0,
    )
    alpha, _, inverse = factor_of_sums(summed)
    alphas[...] = found[...]
    alphas[STEPS - 1] = alpha
    following[...] = mix(inverse, rest[...] - dot_tn(alpha, current[...]))


def last(parts, rest, current, found, total):
    return pl.pallas_call(
        functools.partial(last_kernel, total),
        out_shape=(
            jax.ShapeDtypeStruct(found.shape, F32),
            jax.ShapeDtypeStruct(current.shape, F32),
        ),
        in_specs=[VMEM] * 4,
        out_specs=(VMEM, VMEM),
        compiler_params=PARAMS,
        name="last_block",
    )(parts, rest, current, found)


def swap(blocks, axis, groups=None):
    return lax.all_to_all(blocks, axis, 0, 0, tiled=True, axis_index_groups=groups)


def lines_and_rest(n_row, n_col):
    depth = DEPTH if n_col % DEPTH == 0 else n_col
    lines = [
        [(chip + core) * n_col + high + z for core in range(2) for z in range(depth)]
        for chip in range(0, n_row, 2)
        for high in range(0, n_col, depth)
    ]
    return lines, [list(rest) for rest in zip(*lines)]


def shards(tiles, tile_row, tile_col, tile_count, block, previous, coupling):
    slots = tiles.shape[0]
    sub = block.shape[1]
    n_row = lax.axis_size("row")
    n_col = lax.axis_size("col")
    total = float(sub * n_row * n_col)
    squares = tiles.reshape(slots, TILE, TILE)
    live = lax.iota(jnp.int32, slots) < tile_count[0]
    rows = jnp.where(live, tile_row, n_col * sub // TILE)
    cols = jnp.where(live, tile_col, n_row * sub // TILE)
    lines, others = lines_and_rest(n_row, n_col)

    copies = jnp.broadcast_to(block[None], (n_row, NV, sub))
    band = swap(copies, "row")
    before = swap(front(rows, cols, squares, band, block, n_col), "col")
    partial, owned = back(rows, cols, squares, before, n_row, sub)
    returned = swap(partial, "row")
    rest, message = carry(owned, returned, block, previous, coupling, n_row)

    got = swap(message, "row")
    moved = swap(whiten(rows, cols, squares, got, rest, n_col), "col")
    partial, owned, current, upper, found = settle(
        rows, cols, squares, moved, before, rest, block, total, n_row
    )
    returned = swap(partial, "row")
    rest, sums = local(owned, returned, current, block, upper, len(lines[0]))
    parts = swap(spread(swap(sums, BOTH, lines), len(others[0])), BOTH, others)
    found, current = last(parts, rest, current, found, total)
    return (current, found)


def solution(mesh):
    in_specs = (
        P(("row", "col"), None),
        P(("row", "col")),
        P(("row", "col")),
        P(("row", "col")),
        P(None, ("row", "col")),
        P(None, ("row", "col")),
        P(),
    )
    out_specs = (P(None, ("row", "col")), P())
    return jax.shard_map(shards, mesh=mesh, in_specs=in_specs, out_specs=out_specs, check_vma=False)
```
